512 devices in a mesh: img: 64 (over z, x), aug: 8 (over y, core).
Axes of the slice: x: 4, y: 4, z: 16, core: 2. Of those that a mesh axis runs over, the one named last changes fastest.
Arguments:
- activations: bfloat16 [64, 8, 197, 768], P('img', 'aug'), may hold values from -8 to 8
- out_grads: bfloat16 [64, 8, 197, 3072], P('img', 'aug'), may hold values from -0.33 to 0.33
- kept_mask: int32 [64, 8], P('img', 'aug'), may hold values from 0 to 1, as said below
- noise_field: float32 [768, 3072], P('img', 'aug'), may hold values from -6 to 6
Outputs:
- clipped_sum: float32 [768, 3072], P('img', 'aug')
- update: float32 [768, 3072], P('img', 'aug')
- norms: float32 [64], P('img')
The draws below stay inside these ranges and needn't reach their ends.
Inputs may be any that keep to these rules, and one draw needn't show every extreme that they name: `kept_mask`: every image keeps at least one of its 8 copies.
All inputs are finite; a program needn't handle non-finite values.
Results may differ from the reference program's by a relative error of at most 0.00035.
Values may be sent and summed in bfloat16 or wider, within the bound.
A program may use at most 64 MiB of HBM per device.

```python
import math
import jax
import jax.numpy as jnp
from jax import lax

D = 768
FF = 3072
S = 197
AUGS = 8
IMAGES = 64


def log_spread(key, shape, low_end, high_end):
    return jnp.exp(jax.random.uniform(key, shape, jnp.float32, math.log(low_end), math.log(high_end)))


def draw_activations(key, part):
    key = jax.random.fold_in(key, 1)
    key_base, key_scale = jax.random.split(key)
    base_draw = jax.random.truncated_normal(key_base, -4.0, 4.0, (IMAGES, AUGS, S, D), jnp.float32)
    row_scale = log_spread(key_scale, (D,), 0.5, 2.0)
    return (base_draw * row_scale).astype(jnp.bfloat16)


def draw_out_grads(key, part):
    key = jax.random.fold_in(key, 2)
    key_base = jax.random.fold_in(key, 0)
    key_image = jax.random.fold_in(key, 2)
    key_column = jax.random.fold_in(key, 3)
    base_draw = jax.random.truncated_normal(key_base, -4.0, 4.0, (IMAGES, AUGS, S, FF), jnp.float32)
    image_scale = log_spread(key_image, (IMAGES, 1, 1, 1), 0.004, 0.04)
    column_scale = log_spread(key_column, (FF,), 0.5, 2.0)
    return (base_draw * image_scale * column_scale).astype(jnp.bfloat16)


def draw_kept_mask(key, part):
    key = jax.random.fold_in(key, 3)
    key_flips, key_place = jax.random.split(key)
    coin_flips = jax.random.randint(key_flips, (IMAGES, AUGS), 0, 2)
    position = jax.random.randint(key_place, (IMAGES, 1), 0, AUGS)
    forced = (jnp.arange(AUGS)[None, :] == position).astype(jnp.int32)
    return jnp.maximum(coin_flips, forced).astype(jnp.int32)


def levels(key, shape, pieces, smallest, top_value):
    level = 1.0
    for dim, shards_of in pieces:
        steps = jax.random.uniform(jax.random.fold_in(jax.random.fold_in(key, 6), dim), (shards_of,), jnp.float32, smallest / len(pieces), top_value / len(pieces))
        level = level * jnp.repeat(jnp.exp(steps), shape[dim] // shards_of).reshape((-1,) + (1,) * (len(shape) - 1 - dim))
    return level


def bell_draw(own_key, shape, width, reach, cuts=(), held_as=jnp.bfloat16):
    array = jax.random.normal(own_key, shape, jnp.float32) * width
    if len(cuts) > 0:
        array = levels(own_key, shape, cuts, -0.22, 0.18) * array
    return jnp.clip(array, min=-reach, max=reach).astype(held_as)


def setup_inputs(seed: int = 0) -> dict:
    keys = jax.random.split(jax.random.key(seed), 5)
    activations = draw_activations(jax.random.fold_in(keys[4], 71), 0)
    out_grads = draw_out_grads(jax.random.fold_in(keys[4], 71), 0)
    kept_mask = draw_kept_mask(jax.random.fold_in(keys[4], 71), 0)
    noise_field = bell_draw(keys[3], (D, FF), 1.0, 6.0, ((0, 64), (1, 8)), jnp.float32)
    return {"activations": activations, "out_grads": out_grads, "kept_mask": kept_mask, "noise_field": noise_field}


def reference(activations, out_grads, kept_mask, noise_field):
    clip_bound = 0.01 * math.sqrt(D * FF * S)
    kept_float = kept_mask.astype(jnp.float32)
    kept_count = lax.optimization_barrier(jnp.sum(kept_float, axis=1))

    def per_image(running, image_data):
        acts_one, grads_one, weights, count_one = image_data
        masked = (acts_one * weights.astype(jnp.bfloat16)[:, None, None]).reshape(AUGS * S, D)
        mean_grad = jnp.dot(masked.T, grads_one.reshape(AUGS * S, FF), preferred_element_type=jnp.float32) / count_one
        norm_value = jnp.sqrt(jnp.sum(mean_grad * mean_grad))
        factor = clip_bound / jnp.maximum(norm_value, clip_bound)
        return (running + factor * mean_grad, norm_value)
    clipped_sum, norms = lax.scan(per_image, jnp.zeros((D, FF), jnp.float32), (activations, out_grads, kept_float, kept_count))
    update = (clipped_sum + clip_bound * noise_field) / IMAGES
    return (clipped_sum, update, norms)
```

```python
import functools
import math

import jax
import jax.numpy as jnp
from jax import lax
from jax.experimental import pallas as pl
from jax.experimental.pallas import tpu as pltpu
from jax.sharding import PartitionSpec as P

MESH = pl.DeviceIdType.MESH
NZ, NX, NY = 16, 4, 4
S, D, FF = 197, 768, 3072
SP = 208
SLOT = 256
BW = FF // 8
CH = 3
CW = BW // CH
XR = D // NX
ZR = D // (NX * NZ)
HALF = 112
IMAGES = 64
CLIP = 0.01 * math.sqrt(D * FF * S)
LEVELS = 32766.0


def kernel(
    a_ref, g_ref, m_ref, n_ref,
    clip_ref, upd_ref, norm_ref,
    a_all, a_t, g_pad, g_all, perm, prod, x_in, parts, stat_out, stat_in, fac_out, fac_in, z_out, z_in,
    a_send, a_recv, g_send, g_recv, x_send, x_recv, s_send, s_recv, f_send, f_recv, z_send, z_recv, own_sem,
):
    img, aug = lax.axis_index("img"), lax.axis_index("aug")
    z, x, y, c = img // NX, lax.rem(img, NX), aug // 2, lax.rem(aug, 2)

    def at_y(dy, dc):
        return (img, lax.rem(y + dy, NY) * 2 + (lax.rem(c + dc, 2)))

    def at_x(dx):
        return (z * NX + lax.rem(x + dx, NX), aug)

    def at_z(dz):
        return (lax.rem(z + dz, NZ) * NX + x, aug)

    aug_peers = [(dy, dc) for dy in range(NY) for dc in range(2) if (dy, dc) != (0, 0)]

    barrier = pltpu.get_barrier_semaphore()
    for dy, dc in aug_peers:
        pl.semaphore_signal(barrier, inc=1, device_id=at_y(dy, dc), device_id_type=MESH)
    for dx in range(1, NX):
        pl.semaphore_signal(barrier, inc=1, device_id=at_x(dx), device_id_type=MESH)
    for dz in range(1, NZ):
        pl.semaphore_signal(barrier, inc=1, device_id=at_z(dz), device_id_type=MESH)

    mask = m_ref[...].astype(jnp.float32)
    tail = S - 192
    a_all[0:192, :] = (a_ref[0:192, :].astype(jnp.float32) * mask).astype(jnp.bfloat16)
    a_all[192:SLOT, :] = jnp.zeros((SLOT - 192, D), jnp.bfloat16)
    a_all[192:S, :] = (a_ref[192:S, :].astype(jnp.float32) * mask).astype(jnp.bfloat16)
    g_pad[0:192, :] = g_ref[0:192, :]
    g_pad[192:SP, :] = jnp.zeros((SP - 192, FF), jnp.bfloat16)
    g_pad[192:S, :] = g_ref[192:S, :]
    for s in range(8):
        if s:
            a_all[s * SLOT + SP:(s + 1) * SLOT, :] = jnp.zeros((SLOT - SP, D), jnp.bfloat16)
        g_all[s * SLOT + SP:(s + 1) * SLOT, :] = jnp.zeros((SLOT - SP, BW), jnp.bfloat16)

    p = lax.broadcasted_iota(jnp.int32, (D, 1), 0)
    px, pz, pr = p // XR, lax.rem(p, XR) // ZR, lax.rem(p, ZR)
    source = pz * (NX * ZR) + px * ZR + pr
    perm[...] = (lax.broadcasted_iota(jnp.int32, (D, D), 1) == source).astype(jnp.bfloat16)

    pl.semaphore_wait(barrier, 7 + (NX - 1) + (NZ - 1))

    def a_copy(i, src, dst, rows, device):
        return pltpu.make_async_remote_copy(
            src_ref=a_all.at[pl.ds(src, rows)], dst_ref=a_all.at[pl.ds(dst, rows)],
            send_sem=a_send.at[i], recv_sem=a_recv.at[i], device_id=device, device_id_type=MESH)

    def slot(dy, dc):
        return (dy * 2 + dc) * SLOT

    up = a_copy(0, 0, slot(1, 0), SP, at_y(1, 0))
    down = a_copy(1, 0, slot(3, 0), SP, at_y(3, 0))
    side = a_copy(2, 0, slot(0, 1), SP, at_y(0, 1))
    up.start()
    down.start()
    side.start()

    own_block = pl.ds(pl.multiple_of(aug * BW, BW), BW)
    own_copy = pltpu.make_async_copy(g_pad.at[:, own_block], g_all.at[pl.ds(0, SP)], own_sem)
    own_copy.start()

    g_copies = [[] for _ in range(CH)]

    def start_g(k):
        for i, (dy, dc) in enumerate([(1, 0), (3, 0), (1, 1), (3, 1), (2, 0), (2, 1), (0, 1)]):
            to = lax.rem(y + dy, NY) * 2 + lax.rem(c + dc, 2)
            copy = pltpu.make_async_remote_copy(
                src_ref=g_pad.at[:, pl.ds(pl.multiple_of(to * BW + k * CW, CW), CW)],
                dst_ref=g_all.at[pl.ds(slot(dy, dc), SP), pl.ds(k * CW, CW)],
                send_sem=g_send.at[k, i], recv_sem=g_recv.at[k, i], device_id=at_y(dy, dc), device_id_type=MESH)
            copy.start()
            g_copies[k].append(copy)

    def transpose(s):
        a_t[:, s * SLOT:(s + 1) * SLOT] = lax.dot_general(
            perm[...], a_all[s * SLOT:(s + 1) * SLOT, :], (((1,), (1,)), ((), ())),
            preferred_element_type=jnp.float32).astype(jnp.bfloat16)

    start_g(0)
    transpose(0)
    up.wait_recv()
    far_up = a_copy(3, slot(1, 0), slot(2, 0), HALF, at_y(1, 0))
    far_up.start()
    side_up = a_copy(4, slot(1, 0), slot(1, 1), SP, at_y(0, 1))
    side_up.start()
    down.wait_recv()
    far_down = a_copy(5, slot(3, 0) + HALF, slot(2, 0) + HALF, SP - HALF, at_y(3, 0))
    far_down.start()
    side_down = a_copy(6, slot(3, 0), slot(3, 1), SP, at_y(0, 1))
    side_down.start()
    start_g(1)
    start_g(2)
    side.wait_recv()
    transpose(1)
    transpose(2)
    transpose(6)
    far_up.wait_recv()
    far_down.wait_recv()
    side_far = a_copy(7, slot(2, 0), slot(2, 1), SP, at_y(0, 1))
    side_far.start()
    transpose(4)
    side_up.wait_recv()
    transpose(3)
    side_down.wait_recv()
    transpose(7)
    side_far.wait_recv()
    transpose(5)
    own_copy.wait()

    x_copies = [[] for _ in range(CH)]
    total = jnp.zeros((1, CW), jnp.float32)
    for k in range(CH):
        for copy in g_copies[k]:
            copy.wait_recv()
        cols = slice(k * CW, (k + 1) * CW)
        block = jnp.dot(a_t[...], g_all[:, cols], preferred_element_type=jnp.float32)
        prod[:, cols] = block
        for dx in range(1, NX):
            to = lax.rem(x + dx, NX)
            copy = pltpu.make_async_remote_copy(
                src_ref=prod.at[pl.ds(pl.multiple_of(to * XR, XR), XR), pl.ds(k * CW, CW)],
                dst_ref=x_in.at[dx - 1, :, pl.ds(k * CW, CW)],
                send_sem=x_send.at[k, dx - 1], recv_sem=x_recv.at[k, dx - 1], device_id=at_x(dx), device_id_type=MESH)
            copy.start()
            x_copies[k].append(copy)
        total = total + jnp.sum(block * block, axis=0, keepdims=True)

    square = jnp.sum(total, axis=1, keepdims=True)
    row = lax.broadcasted_iota(jnp.int32, (8, 128), 0)
    stat = jnp.where(row < 4, jnp.broadcast_to(square, (8, 128)), jnp.broadcast_to(mask, (8, 128)))
    stat_out[...] = stat
    s_copies = []
    for i, (dy, dc) in enumerate(aug_peers):
        copy = pltpu.make_async_remote_copy(
            src_ref=stat_out, dst_ref=stat_in.at[i], send_sem=s_send.at[i], recv_sem=s_recv.at[i],
            device_id=at_y(dy, dc), device_id_type=MESH)
        copy.start()
        s_copies.append(copy)
    for copy in s_copies:
        copy.wait_recv()
    near = (stat + stat_in[0]) + (stat_in[3] + stat_in[4])
    far = (stat_in[1] + stat_in[2]) + (stat_in[5] + stat_in[6])
    stat = near + far
    count = stat[4:5, :]
    norm = jnp.sqrt(stat[0:1, :]) / count
    factor = CLIP / jnp.maximum(norm, CLIP)
    weight = factor / count
    norm_ref[...] = norm[:, 0:1]
    fac_out[...] = jnp.broadcast_to(weight, (8, 128))
    f_copies = []
    for dx in range(1, NX):
        copy = pltpu.make_async_remote_copy(
            src_ref=fac_out, dst_ref=fac_in.at[dx - 1], send_sem=f_send.at[dx - 1], recv_sem=f_recv.at[dx - 1],
            device_id=at_x(dx), device_id_type=MESH)
        copy.start()
        f_copies.append(copy)

    own_rows = pl.ds(pl.multiple_of(x * XR, XR), XR)
    for k in range(CH):
        cols = slice(k * CW, (k + 1) * CW)
        parts[:, cols] = weight * prod[own_rows, cols]
    for dx in range(1, NX):
        f_copies[dx - 1].wait_recv()
        far = fac_in[dx - 1, 0:1, :]
        for k in range(CH):
            x_copies[k][dx - 1].wait_recv()
            cols = slice(k * CW, (k + 1) * CW)
            parts[:, cols] += far * x_in[dx - 1, :, cols]

    def scale_of(level):
        return jnp.exp2(level.astype(jnp.float32) * (1.0 / 64.0))

    row8 = lax.broadcasted_iota(jnp.int32, (8, BW), 0)
    for d in range(NZ):
        piece = parts[d * ZR:(d + 1) * ZR, :]
        top = jnp.maximum(jnp.max(jnp.abs(piece), axis=0, keepdims=True), 1e-30)
        level = jnp.ceil(jnp.log2(top) * 64.0).astype(jnp.int32) + 1
        ints = jnp.round(piece * (LEVELS / scale_of(level))).astype(jnp.int32)
        z_out[d, 0:6, :] = ints[0:6] * 65536 + ints[6:12]
        z_out[d, 6:8, :] = jnp.broadcast_to(level, (2, BW))
    z_copies = []
    for d in range(1, NZ):
        copy = pltpu.make_async_remote_copy(
            src_ref=z_out.at[lax.rem(z + d, NZ)], dst_ref=z_in.at[d - 1], send_sem=z_send.at[d - 1], recv_sem=z_recv.at[d - 1],
            device_id=at_z(d), device_id_type=MESH)
        copy.start()
        z_copies.append(copy)

    def unpack(words):
        high = (words[0:6] + 32768) >> 16
        low = words[0:6] - high * 65536
        scale = scale_of(words[6:7]) * (1.0 / LEVELS)
        return high.astype(jnp.float32) * scale, low.astype(jnp.float32) * scale

    top_rows, low_rows = unpack(z_out[z])
    for d in range(1, NZ):
        z_copies[d - 1].wait_recv()
        one, two = unpack(z_in[d - 1])
        top_rows = top_rows + one
        low_rows = low_rows + two
    clip_ref[0:6, :] = top_rows
    clip_ref[6:12, :] = low_rows
    clipped = clip_ref[...]
    upd_ref[...] = (clipped + CLIP * n_ref[...]) * (1.0 / IMAGES)

    for copy in [up, down, side, far_up, side_up, far_down, side_down, side_far]:
        copy.wait_send()
    for copy in sum(g_copies, []) + sum(x_copies, []) + s_copies + f_copies + z_copies:
        copy.wait_send()


def per_device(activations, out_grads, kept_mask, noise_field):
    vmem = pl.BlockSpec(memory_space=pltpu.VMEM)
    dma = pltpu.SemaphoreType.DMA
    bf16, f32 = jnp.bfloat16, jnp.float32
    clipped, update, norm = pl.pallas_call(
        kernel,
        out_shape=(
            jax.ShapeDtypeStruct((ZR, BW), f32), jax.ShapeDtypeStruct((ZR, BW), f32), jax.ShapeDtypeStruct((1, 1), f32)),
        in_specs=[vmem] * 4,
        out_specs=(vmem,) * 3,
        scratch_shapes=[
            pltpu.VMEM((8 * SLOT, D), bf16),
            pltpu.VMEM((D, 8 * SLOT), bf16),
            pltpu.VMEM((SP, FF), bf16),
            pltpu.VMEM((8 * SLOT, BW), bf16),
            pltpu.VMEM((D, D), bf16),
            pltpu.VMEM((D, BW), f32),
            pltpu.VMEM((NX - 1, XR, BW), f32),
            pltpu.VMEM((XR, BW), f32),
            pltpu.VMEM((8, 128), f32),
            pltpu.VMEM((7, 8, 128), f32),
            pltpu.VMEM((8, 128), f32),
            pltpu.VMEM((NX - 1, 8, 128), f32),
            pltpu.VMEM((NZ, 8, BW), jnp.int32),
            pltpu.VMEM((NZ - 1, 8, BW), jnp.int32),
            dma((8,)), dma((8,)), dma((CH, 7)), dma((CH, 7)), dma((CH, NX - 1)), dma((CH, NX - 1)),
            dma((7,)), dma((7,)), dma((NX - 1,)), dma((NX - 1,)), dma((NZ - 1,)), dma((NZ - 1,)), dma,
        ],
        compiler_params=pltpu.CompilerParams(collective_id=0, has_side_effects=True, vmem_limit_bytes=40 * 2**20),
        name="clipped_sum",
    )(activations[0, 0], out_grads[0, 0], kept_mask, noise_field)
    return clipped, update, norm.reshape(1)


def solution(mesh):
    in_specs = (
        P("img", "aug", None, None),
        P("img", "aug", None, None),
        P("img", "aug"),
        P("img", "aug"),
    )
    out_specs = (P("img", "aug"), P("img", "aug"), P("img"))
    return jax.shard_map(
        per_device, mesh=mesh, in_specs=in_specs, out_specs=out_specs, check_vma=False
    )
```

```python
import functools
import math

import jax
import jax.numpy as jnp
from jax import lax
from jax.experimental import pallas as pl
from jax.experimental.pallas import tpu as pltpu
from jax.sharding import PartitionSpec as P

MESH = pl.DeviceIdType.MESH
NZ, NX, NY = 16, 4, 4
S, D, FF = 197, 768, 3072
SP = 208
BW = FF // 8
CH = 3
CW = BW // CH
XR = D // NX
ZR = D // (NX * NZ)
HALF = 112
IMAGES = 64
CLIP = 0.01 * math.sqrt(D * FF * S)
LEVELS = 32766.0


def kernel(
    a_hbm, g_hbm, m_ref, n_hbm,
    clip_ref, upd_ref, norm_ref,
    a_raw, g_raw, noise, a_all, a_perm, g_pad, g_all, perm, prod, x_out, x_in, parts,
    stat_out, stat_in, fac_out, fac_in, z_out, z_in,
    in_sem, a_send, a_recv, g_send, g_recv, x_send, x_recv, s_send, s_recv, f_send, f_recv, z_send, z_recv, own_sem,
):
    img, aug = lax.axis_index("img"), lax.axis_index("aug")
    z, x, y, c = img // NX, lax.rem(img, NX), aug // 2, lax.rem(aug, 2)

    def at_y(dy, dc):
        return (img, lax.rem(y + dy, NY) * 2 + (lax.rem(c + dc, 2)))

    def at_x(dx):
        return (z * NX + lax.rem(x + dx, NX), aug)

    def at_z(dz):
        return (lax.rem(z + dz, NZ) * NX + x, aug)

    aug_peers = [(dy, dc) for dy in range(NY) for dc in range(2) if (dy, dc) != (0, 0)]

    barrier = pltpu.get_barrier_semaphore()
    for dy, dc in aug_peers:
        pl.semaphore_signal(barrier, inc=1, device_id=at_y(dy, dc), device_id_type=MESH)
    for dx in range(1, NX):
        pl.semaphore_signal(barrier, inc=1, device_id=at_x(dx), device_id_type=MESH)
    for dz in range(1, NZ):
        pl.semaphore_signal(barrier, inc=1, device_id=at_z(dz), device_id_type=MESH)

    a_load = pltpu.make_async_copy(a_hbm, a_raw, in_sem.at[0])
    g_load = pltpu.make_async_copy(g_hbm, g_raw, in_sem.at[1])
    n_load = pltpu.make_async_copy(n_hbm, noise, in_sem.at[2])
    a_load.start()
    g_load.start()
    n_load.start()

    p = lax.broadcasted_iota(jnp.int32, (1, D), 1)
    px, pz, pr = p // XR, lax.rem(p, XR) // ZR, lax.rem(p, ZR)
    source = pz * (NX * ZR) + px * ZR + pr
    perm[...] = (lax.broadcasted_iota(jnp.int32, (D, D), 0) == source).astype(jnp.bfloat16)

    mask = m_ref[...].astype(jnp.float32)
    a_load.wait()
    a_all[0:192, :] = (a_raw[0:192, :].astype(jnp.float32) * mask).astype(jnp.bfloat16)
    a_all[192:SP, :] = jnp.zeros((SP - 192, D), jnp.bfloat16)
    a_all[192:S, :] = (a_raw[192:S, :].astype(jnp.float32) * mask).astype(jnp.bfloat16)

    pl.semaphore_wait(barrier, 7 + (NX - 1) + (NZ - 1))

    def a_copy(i, src, dst, first, rows, device):
        return pltpu.make_async_remote_copy(
            src_ref=a_all.at[pl.ds(src * SP + first, rows)], dst_ref=a_all.at[pl.ds(dst * SP + first, rows)],
            send_sem=a_send.at[i], recv_sem=a_recv.at[i], device_id=device, device_id_type=MESH)

    up_far = a_copy(0, 0, 2, 0, HALF, at_y(1, 0))
    down_far = a_copy(1, 0, 6, HALF, SP - HALF, at_y(3, 0))
    up_near = a_copy(2, 0, 2, HALF, SP - HALF, at_y(1, 0))
    down_near = a_copy(3, 0, 6, 0, HALF, at_y(3, 0))
    side = a_copy(4, 0, 1, 0, SP, at_y(0, 1))
    a_copies = [up_far, down_far, up_near, down_near, side]
    for copy in a_copies:
        copy.start()

    g_load.wait()
    g_pad[0:192, :] = g_raw[0:192, :]
    g_pad[192:SP, :] = jnp.zeros((SP - 192, FF), jnp.bfloat16)
    g_pad[192:S, :] = g_raw[192:S, :]
    own_block = pl.ds(pl.multiple_of(aug * BW, BW), BW)
    own_copy = pltpu.make_async_copy(g_pad.at[:, own_block], g_all.at[pl.ds(0, SP)], own_sem)
    own_copy.start()

    up_far.wait_recv()
    far_up = a_copy(5, 2, 4, 0, HALF, at_y(1, 0))
    far_up.start()
    down_far.wait_recv()
    far_down = a_copy(6, 6, 4, HALF, SP - HALF, at_y(3, 0))
    far_down.start()

    g_copies = [[] for _ in range(CH)]
    for k in range(CH):
        for i, (dy, dc) in enumerate([(1, 0), (3, 0), (1, 1), (3, 1), (2, 0), (2, 1), (0, 1)]):
            to = lax.rem(y + dy, NY) * 2 + lax.rem(c + dc, 2)
            copy = pltpu.make_async_remote_copy(
                src_ref=g_pad.at[:, pl.ds(pl.multiple_of(to * BW + k * CW, CW), CW)],
                dst_ref=g_all.at[pl.ds((dy * 2 + dc) * SP, SP), pl.ds(k * CW, CW)],
                send_sem=g_send.at[k, i], recv_sem=g_recv.at[k, i], device_id=at_y(dy, dc), device_id_type=MESH)
            copy.start()
            g_copies[k].append(copy)

    def permute(s):
        rows = slice(s * SP, (s + 1) * SP)
        a_perm[rows, :] = jnp.dot(a_all[rows, :], perm[...], preferred_element_type=jnp.float32).astype(jnp.bfloat16)

    up_near.wait_recv()
    side_up = a_copy(7, 2, 3, 0, SP, at_y(0, 1))
    side_up.start()
    down_near.wait_recv()
    side_down = a_copy(8, 6, 7, 0, SP, at_y(0, 1))
    side_down.start()
    permute(0)
    side.wait_recv()
    permute(1)
    permute(2)
    permute(6)
    far_up.wait_recv()
    far_down.wait_recv()
    side_far = a_copy(9, 4, 5, 0, SP, at_y(0, 1))
    side_far.start()
    permute(4)
    side_up.wait_recv()
    permute(3)
    side_down.wait_recv()
    permute(7)
    side_far.wait_recv()
    permute(5)
    a_copies += [far_up, far_down, side_up, side_down, side_far]
    own_copy.wait()

    def scale_of(level):
        return jnp.exp2(level.astype(jnp.float32) * (1.0 / 64.0))

    def pack(piece):
        half = piece.shape[0] // 2
        top = jnp.maximum(jnp.max(jnp.abs(piece), axis=0, keepdims=True), 1e-30)
        level = jnp.ceil(jnp.log2(top) * 64.0).astype(jnp.int32) + 1
        ints = jnp.round(piece * (LEVELS / scale_of(level))).astype(jnp.int32)
        return ints[:half] * 65536 + ints[half:], level

    def unpack(words, level, weight):
        high = (words + 32768) >> 16
        low = words - high * 65536
        scale = scale_of(level) * (weight * (1.0 / LEVELS))
        return high.astype(jnp.float32) * scale, low.astype(jnp.float32) * scale

    x_copies = [[] for _ in range(CH)]
    total = jnp.zeros((1, CW), jnp.float32)
    for k in range(CH):
        for copy in g_copies[k]:
            copy.wait_recv()
        cols = slice(k * CW, (k + 1) * CW)
        block = lax.dot_general(
            a_perm[...], g_all[:, cols], (((0,), (0,)), ((), ())), preferred_element_type=jnp.float32)
        prod[:, cols] = block
        for t in range(NX):
            words, level = pack(block[t * XR:(t + 1) * XR])
            x_out[k, t, 0:XR // 2, :] = words
            x_out[k, t, XR // 2:, :] = jnp.broadcast_to(level, (8, CW))
        for dx in range(1, NX):
            copy = pltpu.make_async_remote_copy(
                src_ref=x_out.at[k, lax.rem(x + dx, NX)], dst_ref=x_in.at[k, dx - 1],
                send_sem=x_send.at[k, dx - 1], recv_sem=x_recv.at[k, dx - 1], device_id=at_x(dx), device_id_type=MESH)
            copy.start()
            x_copies[k].append(copy)
        total = total + jnp.sum(block * block, axis=0, keepdims=True)

    square = jnp.sum(total, axis=1, keepdims=True)
    row = lax.broadcasted_iota(jnp.int32, (8, 128), 0)
    stat = jnp.where(row < 4, jnp.broadcast_to(square, (8, 128)), jnp.broadcast_to(mask, (8, 128)))
    stat_out[...] = stat
    s_copies = []
    for i, (dy, dc) in enumerate(aug_peers):
        copy = pltpu.make_async_remote_copy(
            src_ref=stat_out, dst_ref=stat_in.at[i], send_sem=s_send.at[i], recv_sem=s_recv.at[i],
            device_id=at_y(dy, dc), device_id_type=MESH)
        copy.start()
        s_copies.append(copy)
    for copy in s_copies:
        copy.wait_recv()
    near = (stat + stat_in[0]) + (stat_in[3] + stat_in[4])
    far = (stat_in[1] + stat_in[2]) + (stat_in[5] + stat_in[6])
    stat = near + far
    count = stat[4:5, :]
    norm = jnp.sqrt(stat[0:1, :]) / count
    factor = CLIP / jnp.maximum(norm, CLIP)
    weight = factor / count
    norm_ref[...] = norm[:, 0:1]
    fac_out[...] = jnp.broadcast_to(weight, (8, 128))
    f_copies = []
    for dx in range(1, NX):
        copy = pltpu.make_async_remote_copy(
            src_ref=fac_out, dst_ref=fac_in.at[dx - 1], send_sem=f_send.at[dx - 1], recv_sem=f_recv.at[dx - 1],
            device_id=at_x(dx), device_id_type=MESH)
        copy.start()
        f_copies.append(copy)

    own_rows = pl.ds(pl.multiple_of(x * XR, XR), XR)
    for k in range(CH):
        cols = slice(k * CW, (k + 1) * CW)
        parts[:, cols] = weight * prod[own_rows, cols]
    for copy in f_copies:
        copy.wait_recv()
    half = XR // 2
    for k in range(CH):
        cols = slice(k * CW, (k + 1) * CW)
        high, low = parts[0:half, cols], parts[half:, cols]
        for d in range(NX - 1):
            x_copies[k][d].wait_recv()
            one, two = unpack(x_in[k, d, 0:half, :], x_in[k, d, half:half + 1, :], fac_in[d, 0:1, :])
            high = high + one
            low = low + two
        parts[0:half, cols] = high
        parts[half:, cols] = low

    for d in range(NZ):
        words, level = pack(parts[d * ZR:(d + 1) * ZR, :])
        z_out[d, 0:6, :] = words
        z_out[d, 6:8, :] = jnp.broadcast_to(level, (2, BW))
    z_copies = []
    for d in range(1, NZ):
        copy = pltpu.make_async_remote_copy(
            src_ref=z_out.at[lax.rem(z + d, NZ)], dst_ref=z_in.at[d - 1], send_sem=z_send.at[d - 1], recv_sem=z_recv.at[d - 1],
            device_id=at_z(d), device_id_type=MESH)
        copy.start()
        z_copies.append(copy)

    own = z_out[z]
    top_rows, low_rows = unpack(own[0:6], own[6:7], 1.0)
    for d in range(1, NZ):
        z_copies[d - 1].wait_recv()
        words = z_in[d - 1]
        one, two = unpack(words[0:6], words[6:7], 1.0)
        top_rows = top_rows + one
        low_rows = low_rows + two
    n_load.wait()
    clip_ref[0:6, :] = top_rows
    clip_ref[6:12, :] = low_rows
    upd_ref[0:6, :] = (top_rows + CLIP * noise[0:6, :]) * (1.0 / IMAGES)
    upd_ref[6:12, :] = (low_rows + CLIP * noise[6:12, :]) * (1.0 / IMAGES)

    for copy in a_copies + sum(g_copies, []) + sum(x_copies, []) + s_copies + f_copies + z_copies:
        copy.wait_send()


def per_device(activations, out_grads, kept_mask, noise_field):
    vmem = pl.BlockSpec(memory_space=pltpu.VMEM)
    hbm = pl.BlockSpec(memory_space=pl.ANY)
    dma = pltpu.SemaphoreType.DMA
    bf16, f32, i32 = jnp.bfloat16, jnp.float32, jnp.int32
    clipped, update, norm = pl.pallas_call(
        kernel,
        out_shape=(
            jax.ShapeDtypeStruct((ZR, BW), f32), jax.ShapeDtypeStruct((ZR, BW), f32), jax.ShapeDtypeStruct((1, 1), f32)),
        in_specs=[hbm, hbm, vmem, hbm],
        out_specs=(vmem,) * 3,
        scratch_shapes=[
            pltpu.VMEM((S, D), bf16),
            pltpu.VMEM((S, FF), bf16),
            pltpu.VMEM((ZR, BW), f32),
            pltpu.VMEM((8 * SP, D), bf16),
            pltpu.VMEM((8 * SP, D), bf16),
            pltpu.VMEM((SP, FF), bf16),
            pltpu.VMEM((8 * SP, BW), bf16),
            pltpu.VMEM((D, D), bf16),
            pltpu.VMEM((D, BW), f32),
            pltpu.VMEM((CH, NX, XR // 2 + 8, CW), i32),
            pltpu.VMEM((CH, NX - 1, XR // 2 + 8, CW), i32),
            pltpu.VMEM((XR, BW), f32),
            pltpu.VMEM((8, 128), f32),
            pltpu.VMEM((7, 8, 128), f32),
            pltpu.VMEM((8, 128), f32),
            pltpu.VMEM((NX - 1, 8, 128), f32),
            pltpu.VMEM((NZ, 8, BW), i32),
            pltpu.VMEM((NZ - 1, 8, BW), i32),
            dma((3,)), dma((10,)), dma((10,)), dma((CH, 7)), dma((CH, 7)), dma((CH, NX - 1)), dma((CH, NX - 1)),
            dma((7,)), dma((7,)), dma((NX - 1,)), dma((NX - 1,)), dma((NZ - 1,)), dma((NZ - 1,)), dma,
        ],
        compiler_params=pltpu.CompilerParams(collective_id=0, has_side_effects=True, vmem_limit_bytes=56 * 2**20),
        name="clipped_sum",
    )(activations[0, 0], out_grads[0, 0], kept_mask, noise_field)
    return clipped, update, norm.reshape(1)


def solution(mesh):
    in_specs = (
        P("img", "aug", None, None),
        P("img", "aug", None, None),
        P("img", "aug"),
        P("img", "aug"),
    )
    out_specs = (P("img", "aug"), P("img", "aug"), P("img"))
    return jax.shard_map(
        per_device, mesh=mesh, in_specs=in_specs, out_specs=out_specs, check_vma=False
    )
```

```python
import functools
import math

import jax
import jax.numpy as jnp
from jax import lax
from jax.experimental import pallas as pl
from jax.experimental.pallas import tpu as pltpu
from jax.sharding import PartitionSpec as P

MESH = pl.DeviceIdType.MESH
NZ, NX, NY = 16, 4, 4
S, D, FF = 197, 768, 3072
SP = 208
BW = FF // 8
CH = 3
CW = BW // CH
XR = D // NX
ZR = D // (NX * NZ)
HALF = 112
IMAGES = 64
CLIP = 0.01 * math.sqrt(D * FF * S)
LEVELS = 32766.0
X_ORDER = (2, 1, 3, 0)
Z_ORDER = (8, 7, 9, 6, 10, 5, 11, 4, 12, 3, 13, 2, 14, 1, 15, 0)


def kernel(
    a_hbm, g_hbm, m_ref,
    own_ref, rest_ref, norm_ref,
    a_raw, g_raw, a_all, a_perm, g_pad, g_all, perm, own_part, x_out, x_in, parts,
    stat_out, stat_in, fac_out, fac_in, z_out, z_in,
    in_sem, a_send, a_recv, g_send, g_recv, x_send, x_recv, s_send, s_recv, f_send, f_recv, z_send, z_recv, own_sem, met,
):
    img, aug = lax.axis_index("img"), lax.axis_index("aug")
    z, x, y, c = img // NX, lax.rem(img, NX), aug // 2, lax.rem(aug, 2)

    def at_y(dy, dc):
        return (img, lax.rem(y + dy, NY) * 2 + (lax.rem(c + dc, 2)))

    def at_x(dx):
        return (z * NX + lax.rem(x + dx, NX), aug)

    def at_z(dz):
        return (lax.rem(z + dz + NZ, NZ) * NX + x, aug)

    same_core = [(1, 0), (3, 0), (2, 0)]
    other_core = [(0, 1), (1, 1), (3, 1), (2, 1)]
    aug_peers = [(dy, dc) for dy in range(NY) for dc in range(2) if (dy, dc) != (0, 0)]

    barrier = pltpu.get_barrier_semaphore()
    for dy, dc in aug_peers:
        pl.semaphore_signal(barrier, inc=1, device_id=at_y(dy, dc), device_id_type=MESH)
    for dx in range(1, NX):
        pl.semaphore_signal(barrier, inc=1, device_id=at_x(dx), device_id_type=MESH)
    for dz in (1, -1):
        pl.semaphore_signal(barrier, inc=1, device_id=at_z(dz), device_id_type=MESH)

    a_load = pltpu.make_async_copy(a_hbm, a_raw, in_sem.at[0])
    g_load = pltpu.make_async_copy(g_hbm, g_raw, in_sem.at[1])
    a_load.start()
    g_load.start()

    p = lax.broadcasted_iota(jnp.int32, (1, D), 1)
    px, pz, pr = p // XR, lax.rem(p, XR) // ZR, lax.rem(p, ZR)
    to_x = lax.rem(x + jnp.where(px == 0, 2, jnp.where(px == 3, 0, px * 2 - 1)), NX)
    source = lax.rem(z + pz, NZ) * (NX * ZR) + to_x * ZR + pr
    perm[...] = (lax.broadcasted_iota(jnp.int32, (D, D), 0) == source).astype(jnp.bfloat16)

    mask = m_ref[...].astype(jnp.float32)
    a_load.wait()
    a_all[0:192, :] = (a_raw[0:192, :].astype(jnp.float32) * mask).astype(jnp.bfloat16)
    a_all[192:SP, :] = jnp.zeros((SP - 192, D), jnp.bfloat16)
    a_all[192:S, :] = (a_raw[192:S, :].astype(jnp.float32) * mask).astype(jnp.bfloat16)

    pl.semaphore_wait(barrier, 7 + (NX - 1) + 2)

    def call_z(step):
        for dz in (1 << step, -(1 << step)):
            pl.semaphore_signal(met.at[step], inc=1, device_id=at_z(dz), device_id_type=MESH)

    call_z(0)

    def a_copy(i, src, dst, first, rows, device):
        return pltpu.make_async_remote_copy(
            src_ref=a_all.at[pl.ds(src * SP + first, rows)], dst_ref=a_all.at[pl.ds(dst * SP + first, rows)],
            send_sem=a_send.at[i], recv_sem=a_recv.at[i], device_id=device, device_id_type=MESH)

    up_far = a_copy(0, 0, 2, 0, HALF, at_y(1, 0))
    down_far = a_copy(1, 0, 6, HALF, SP - HALF, at_y(3, 0))
    up_near = a_copy(2, 0, 2, HALF, SP - HALF, at_y(1, 0))
    down_near = a_copy(3, 0, 6, 0, HALF, at_y(3, 0))
    side = a_copy(4, 0, 1, 0, SP, at_y(0, 1))
    a_copies = [up_far, down_far, up_near, down_near]
    for copy in a_copies:
        copy.start()

    pl.semaphore_wait(met.at[0], 2)
    call_z(1)
    g_load.wait()
    g_pad[0:192, :] = g_raw[0:192, :]
    g_pad[192:SP, :] = jnp.zeros((SP - 192, FF), jnp.bfloat16)
    g_pad[192:S, :] = g_raw[192:S, :]
    own_block = pl.ds(pl.multiple_of(aug * BW, BW), BW)
    own_copy = pltpu.make_async_copy(g_pad.at[:, own_block], g_all.at[pl.ds(0, SP)], own_sem)
    own_copy.start()

    up_far.wait_recv()
    far_up = a_copy(5, 2, 4, 0, HALF, at_y(1, 0))
    far_up.start()
    down_far.wait_recv()
    far_down = a_copy(6, 6, 4, HALF, SP - HALF, at_y(3, 0))
    far_down.start()

    g_copies = [[] for _ in range(CH)]

    def start_g(k, peers):
        for dy, dc in peers:
            i = len(g_copies[k])
            to = lax.rem(y + dy, NY) * 2 + lax.rem(c + dc, 2)
            copy = pltpu.make_async_remote_copy(
                src_ref=g_pad.at[:, pl.ds(pl.multiple_of(to * BW + k * CW, CW), CW)],
                dst_ref=g_all.at[pl.ds((dy * 2 + dc) * SP, SP), pl.ds(k * CW, CW)],
                send_sem=g_send.at[k, i], recv_sem=g_recv.at[k, i], device_id=at_y(dy, dc), device_id_type=MESH)
            copy.start()
            g_copies[k].append(copy)

    side.start()
    start_g(0, same_core + other_core)
    start_g(1, same_core + other_core)
    start_g(2, same_core + other_core)

    pl.semaphore_wait(met.at[1], 2)
    call_z(2)

    def permute(s):
        rows = slice(s * SP, (s + 1) * SP)
        a_perm[rows, :] = jnp.dot(a_all[rows, :], perm[...], preferred_element_type=jnp.float32).astype(jnp.bfloat16)

    up_near.wait_recv()
    side_up = a_copy(7, 2, 3, 0, SP, at_y(0, 1))
    side_up.start()
    down_near.wait_recv()
    side_down = a_copy(8, 6, 7, 0, SP, at_y(0, 1))
    side_down.start()
    permute(0)
    side.wait_recv()
    permute(1)
    permute(2)
    permute(6)
    far_up.wait_recv()
    far_down.wait_recv()
    side_far = a_copy(9, 4, 5, 0, SP, at_y(0, 1))
    side_far.start()
    permute(4)
    side_up.wait_recv()
    permute(3)
    side_down.wait_recv()
    permute(7)
    side_far.wait_recv()
    permute(5)
    a_copies += [side, far_up, far_down, side_up, side_down, side_far]
    own_copy.wait()

    def scale_of(level):
        return jnp.exp2(level.astype(jnp.float32) * (1.0 / 64.0))

    def pack(piece):
        half = piece.shape[0] // 2
        top = jnp.maximum(jnp.max(jnp.abs(piece), axis=0, keepdims=True), 1e-30)
        level = jnp.ceil(jnp.log2(top) * 64.0).astype(jnp.int32) + 1
        ints = jnp.round(piece * (LEVELS / scale_of(level))).astype(jnp.int32)
        return ints[:half] * 65536 + ints[half:], level

    def unpack(words, level, weight):
        high = (words + 32768) >> 16
        low = words - high * 65536
        scale = scale_of(level) * (weight * (1.0 / LEVELS))
        return high.astype(jnp.float32) * scale, low.astype(jnp.float32) * scale

    x_copies = [[] for _ in range(CH)]
    total = jnp.zeros((1, CW), jnp.float32)
    for k in range(CH):
        for copy in g_copies[k]:
            copy.wait_recv()
        cols = slice(k * CW, (k + 1) * CW)
        for h in range(2):
            block = lax.dot_general(
                a_perm[:, h * 2 * XR:(h + 1) * 2 * XR], g_all[:, cols], (((0,), (0,)), ((), ())),
                preferred_element_type=jnp.float32)
            total = total + jnp.sum(block * block, axis=0, keepdims=True)
            if h == 1:
                own_part[:, cols] = block[XR:]
            for t in range(2 - h):
                words, level = pack(block[t * XR:(t + 1) * XR])
                n = h * 2 + t
                x_out[k, n, 0:XR // 2, :] = words
                x_out[k, n, XR // 2:, :] = jnp.broadcast_to(level, (8, CW))
                copy = pltpu.make_async_remote_copy(
                    src_ref=x_out.at[k, n], dst_ref=x_in.at[k, n],
                    send_sem=x_send.at[k, n], recv_sem=x_recv.at[k, n], device_id=at_x(X_ORDER[n]), device_id_type=MESH)
                copy.start()
                x_copies[k].append(copy)

    pl.semaphore_wait(met.at[2], 2)

    square = jnp.sum(total, axis=1, keepdims=True)
    row = lax.broadcasted_iota(jnp.int32, (8, 128), 0)
    stat = jnp.where(row < 4, jnp.broadcast_to(square, (8, 128)), jnp.broadcast_to(mask, (8, 128)))
    stat_out[...] = stat
    s_copies = []
    for i, (dy, dc) in enumerate(aug_peers):
        copy = pltpu.make_async_remote_copy(
            src_ref=stat_out, dst_ref=stat_in.at[i], send_sem=s_send.at[i], recv_sem=s_recv.at[i],
            device_id=at_y(dy, dc), device_id_type=MESH)
        copy.start()
        s_copies.append(copy)
    for copy in s_copies:
        copy.wait_recv()
    near = (stat + stat_in[0]) + (stat_in[3] + stat_in[4])
    far = (stat_in[1] + stat_in[2]) + (stat_in[5] + stat_in[6])
    stat = near + far
    count = stat[4:5, :]
    norm = jnp.sqrt(stat[0:1, :]) / count
    factor = CLIP / jnp.maximum(norm, CLIP)
    weight = factor / count
    norm_ref[...] = norm[:, 0:1]
    fac_out[...] = jnp.broadcast_to(weight, (8, 128))
    f_copies = []
    for n in range(NX - 1):
        copy = pltpu.make_async_remote_copy(
            src_ref=fac_out, dst_ref=fac_in.at[n], send_sem=f_send.at[n], recv_sem=f_recv.at[n],
            device_id=at_x(X_ORDER[n]), device_id_type=MESH)
        copy.start()
        f_copies.append(copy)

    for copy in f_copies:
        copy.wait_recv()
    half = XR // 2
    for k in range(CH):
        cols = slice(k * CW, (k + 1) * CW)
        high, low = weight * own_part[0:half, cols], weight * own_part[half:, cols]
        for n in range(NX - 1):
            x_copies[k][n].wait_recv()
            one, two = unpack(x_in[k, n, 0:half, :], x_in[k, n, half:half + 1, :], fac_in[n, 0:1, :])
            high = high + one
            low = low + two
        parts[0:half, cols] = high
        parts[half:, cols] = low

    z_copies = []
    for d in Z_ORDER:
        words, level = pack(parts[d * ZR:(d + 1) * ZR, :])
        if d == 0:
            own_ref[0:6, :], own_ref[6:12, :] = unpack(words, level, 1.0)
            continue
        z_out[d - 1, 0:6, :] = words
        z_out[d - 1, 6:8, :] = jnp.broadcast_to(level, (2, BW))
        copy = pltpu.make_async_remote_copy(
            src_ref=z_out.at[d - 1], dst_ref=z_in.at[d - 1], send_sem=z_send.at[d - 1], recv_sem=z_recv.at[d - 1],
            device_id=at_z(d), device_id_type=MESH)
        copy.start()
        z_copies.append((d, copy))

    top_rows = low_rows = None
    for d, copy in reversed(z_copies):
        copy.wait_recv()
        words = z_in[d - 1]
        one, two = unpack(words[0:6], words[6:7], 1.0)
        top_rows = one if top_rows is None else top_rows + one
        low_rows = two if low_rows is None else low_rows + two
    rest_ref[0:6, :] = top_rows
    rest_ref[6:12, :] = low_rows

    for copy in a_copies + sum(g_copies, []) + sum(x_copies, []) + s_copies + f_copies + [copy for _, copy in z_copies]:
        copy.wait_send()


def per_device(activations, out_grads, kept_mask, noise_field):
    vmem = pl.BlockSpec(memory_space=pltpu.VMEM)
    hbm = pl.BlockSpec(memory_space=pl.ANY)
    dma = pltpu.SemaphoreType.DMA
    bf16, f32, i32 = jnp.bfloat16, jnp.float32, jnp.int32
    own, rest, norm = pl.pallas_call(
        kernel,
        out_shape=(
            jax.ShapeDtypeStruct((ZR, BW), f32), jax.ShapeDtypeStruct((ZR, BW), f32), jax.ShapeDtypeStruct((1, 1), f32)),
        in_specs=[hbm, hbm, vmem],
        out_specs=(vmem,) * 3,
        scratch_shapes=[
            pltpu.VMEM((S, D), bf16),
            pltpu.VMEM((S, FF), bf16),
            pltpu.VMEM((8 * SP, D), bf16),
            pltpu.VMEM((8 * SP, D), bf16),
            pltpu.VMEM((SP, FF), bf16),
            pltpu.VMEM((8 * SP, BW), bf16),
            pltpu.VMEM((D, D), bf16),
            pltpu.VMEM((XR, BW), f32),
            pltpu.VMEM((CH, NX - 1, XR // 2 + 8, CW), i32),
            pltpu.VMEM((CH, NX - 1, XR // 2 + 8, CW), i32),
            pltpu.VMEM((XR, BW), f32),
            pltpu.VMEM((8, 128), f32),
            pltpu.VMEM((7, 8, 128), f32),
            pltpu.VMEM((8, 128), f32),
            pltpu.VMEM((NX - 1, 8, 128), f32),
            pltpu.VMEM((NZ - 1, 8, BW), i32),
            pltpu.VMEM((NZ - 1, 8, BW), i32),
            dma((2,)), dma((10,)), dma((10,)), dma((CH, 7)), dma((CH, 7)), dma((CH, NX - 1)), dma((CH, NX - 1)),
            dma((7,)), dma((7,)), dma((NX - 1,)), dma((NX - 1,)), dma((NZ - 1,)), dma((NZ - 1,)), dma, pltpu.SemaphoreType.REGULAR((3,)),
        ],
        compiler_params=pltpu.CompilerParams(collective_id=0, has_side_effects=True, vmem_limit_bytes=56 * 2**20),
        name="clipped_sum",
    )(activations[0, 0], out_grads[0, 0], kept_mask)
    clipped = own + rest
    update = (clipped + CLIP * noise_field) * (1.0 / IMAGES)
    return clipped, update, norm.reshape(1)


def solution(mesh):
    in_specs = (
        P("img", "aug", None, None),
        P("img", "aug", None, None),
        P("img", "aug"),
        P("img", "aug"),
    )
    out_specs = (P("img", "aug"), P("img", "aug"), P("img"))
    return jax.shard_map(
        per_device, mesh=mesh, in_specs=in_specs, out_specs=out_specs, check_vma=False
    )
```

```python
import functools
import math

import jax
import jax.numpy as jnp
from jax import lax
from jax.experimental import pallas as pl
from jax.experimental.pallas import tpu as pltpu
from jax.sharding import PartitionSpec as P

MESH = pl.DeviceIdType.MESH
NZ, NX, NY = 16, 4, 4
S, D, FF = 197, 768, 3072
SP = 208
BW = FF // 8
CH = 3
CW = BW // CH
XR = D // 8
ZR = D // (NX * NZ)
HALF = 112
IMAGES = 64
CLIP = 0.01 * math.sqrt(D * FF * S)
LEVELS = 32766.0
GROUP = ((2, 1), (2, 0), (1, 1), (1, 0), (3, 1), (3, 0), (0, 1), (0, 0))
Z_ORDER = (4, 3, 5, 2, 6, 1, 7, 0)


def kernel(
    a_hbm, g_hbm, m_ref,
    own_ref, rest_ref, norm_ref,
    a_raw, g_raw, a_all, a_perm, g_pad, g_all, perm, own_part, x_out, x_in, parts,
    stat_out, stat_in, fac_out, fac_in, z_out, z_in,
    in_sem, a_send, a_recv, g_send, g_recv, x_send, x_recv, s_send, s_recv, f_send, f_recv, z_send, z_recv, own_sem, met,
):
    img, aug = lax.axis_index("img"), lax.axis_index("aug")
    z, x, y, c = img // NX, lax.rem(img, NX), aug // 2, lax.rem(aug, 2)

    def at_y(dy, dc):
        return (img, lax.rem(y + dy, NY) * 2 + (lax.rem(c + dc, 2)))

    pair = z + 1 - 2 * lax.rem(z, 2)

    def in_group(dx, other):
        return ((pair if other else z) * NX + lax.rem(x + dx, NX), aug)

    def at_z(dz):
        return (lax.rem(z + dz + NZ, NZ) * NX + x, aug)

    same_core = [(1, 0), (3, 0), (2, 0)]
    other_core = [(0, 1), (1, 1), (3, 1), (2, 1)]
    aug_peers = [(dy, dc) for dy in range(NY) for dc in range(2) if (dy, dc) != (0, 0)]

    barrier = pltpu.get_barrier_semaphore()
    for dy, dc in aug_peers:
        pl.semaphore_signal(barrier, inc=1, device_id=at_y(dy, dc), device_id_type=MESH)
    for dx, other in GROUP[:7]:
        pl.semaphore_signal(barrier, inc=1, device_id=in_group(dx, other), device_id_type=MESH)
    pl.semaphore_signal(barrier, inc=1, device_id=at_z(1 - 2 * lax.rem(z + 1, 2)), device_id_type=MESH)

    a_load = pltpu.make_async_copy(a_hbm, a_raw, in_sem.at[0])
    g_load = pltpu.make_async_copy(g_hbm, g_raw, in_sem.at[1])
    a_load.start()
    g_load.start()

    p = lax.broadcasted_iota(jnp.int32, (1, D), 1)
    pn, pj, pr = p // XR, lax.rem(p, XR) // ZR, lax.rem(p, ZR)
    step_x = jnp.where(pn < 2, 2, jnp.where(pn < 4, 1, jnp.where(pn < 6, 3, 0)))
    from_z = jnp.where(lax.rem(pn, 2) == 0, pair, z)
    source = lax.rem(from_z + 2 * pj, NZ) * (NX * ZR) + lax.rem(x + step_x, NX) * ZR + pr
    perm[...] = (lax.broadcasted_iota(jnp.int32, (D, D), 0) == source).astype(jnp.bfloat16)

    mask = m_ref[...].astype(jnp.float32)
    a_load.wait()
    a_all[0:192, :] = (a_raw[0:192, :].astype(jnp.float32) * mask).astype(jnp.bfloat16)
    a_all[192:SP, :] = jnp.zeros((SP - 192, D), jnp.bfloat16)
    a_all[192:S, :] = (a_raw[192:S, :].astype(jnp.float32) * mask).astype(jnp.bfloat16)

    pl.semaphore_wait(barrier, 7 + 7 + 1)

    def call_z(step):
        for dz in (1 << step, -(1 << step)):
            pl.semaphore_signal(met.at[step], inc=1, device_id=at_z(dz), device_id_type=MESH)

    call_z(0)

    def a_copy(i, src, dst, first, rows, device):
        return pltpu.make_async_remote_copy(
            src_ref=a_all.at[pl.ds(src * SP + first, rows)], dst_ref=a_all.at[pl.ds(dst * SP + first, rows)],
            send_sem=a_send.at[i], recv_sem=a_recv.at[i], device_id=device, device_id_type=MESH)

    up_far = a_copy(0, 0, 2, 0, HALF, at_y(1, 0))
    down_far = a_copy(1, 0, 6, HALF, SP - HALF, at_y(3, 0))
    up_near = a_copy(2, 0, 2, HALF, SP - HALF, at_y(1, 0))
    down_near = a_copy(3, 0, 6, 0, HALF, at_y(3, 0))
    side = a_copy(4, 0, 1, 0, SP, at_y(0, 1))
    a_copies = [up_far, down_far, up_near, down_near]
    for copy in a_copies:
        copy.start()

    pl.semaphore_wait(met.at[0], 2)
    call_z(1)
    g_load.wait()
    g_pad[0:192, :] = g_raw[0:192, :]
    g_pad[192:SP, :] = jnp.zeros((SP - 192, FF), jnp.bfloat16)
    g_pad[192:S, :] = g_raw[192:S, :]
    own_block = pl.ds(pl.multiple_of(aug * BW, BW), BW)
    own_copy = pltpu.make_async_copy(g_pad.at[:, own_block], g_all.at[pl.ds(0, SP)], own_sem)
    own_copy.start()

    up_far.wait_recv()
    far_up = a_copy(5, 2, 4, 0, HALF, at_y(1, 0))
    far_up.start()
    down_far.wait_recv()
    far_down = a_copy(6, 6, 4, HALF, SP - HALF, at_y(3, 0))
    far_down.start()

    g_copies = [[] for _ in range(CH)]

    def start_g(k, peers):
        for dy, dc in peers:
            i = len(g_copies[k])
            to = lax.rem(y + dy, NY) * 2 + lax.rem(c + dc, 2)
            copy = pltpu.make_async_remote_copy(
                src_ref=g_pad.at[:, pl.ds(pl.multiple_of(to * BW + k * CW, CW), CW)],
                dst_ref=g_all.at[pl.ds((dy * 2 + dc) * SP, SP), pl.ds(k * CW, CW)],
                send_sem=g_send.at[k, i], recv_sem=g_recv.at[k, i], device_id=at_y(dy, dc), device_id_type=MESH)
            copy.start()
            g_copies[k].append(copy)

    side.start()
    start_g(0, same_core + other_core)
    start_g(1, same_core + other_core)
    start_g(2, same_core + other_core)

    pl.semaphore_wait(met.at[1], 2)
    call_z(2)

    def permute(s):
        rows = slice(s * SP, (s + 1) * SP)
        a_perm[rows, :] = jnp.dot(a_all[rows, :], perm[...], preferred_element_type=jnp.float32).astype(jnp.bfloat16)

    up_near.wait_recv()
    side_up = a_copy(7, 2, 3, 0, SP, at_y(0, 1))
    side_up.start()
    down_near.wait_recv()
    side_down = a_copy(8, 6, 7, 0, SP, at_y(0, 1))
    side_down.start()
    permute(0)
    side.wait_recv()
    permute(1)
    permute(2)
    permute(6)
    far_up.wait_recv()
    far_down.wait_recv()
    side_far = a_copy(9, 4, 5, 0, SP, at_y(0, 1))
    side_far.start()
    permute(4)
    side_up.wait_recv()
    permute(3)
    side_down.wait_recv()
    permute(7)
    side_far.wait_recv()
    permute(5)
    a_copies += [side, far_up, far_down, side_up, side_down, side_far]
    own_copy.wait()

    def scale_of(level):
        return jnp.exp2(level.astype(jnp.float32) * (1.0 / 64.0))

    def pack(piece):
        half = piece.shape[0] // 2
        top = jnp.maximum(jnp.max(jnp.abs(piece), axis=0, keepdims=True), 1e-30)
        level = jnp.ceil(jnp.log2(top) * 64.0).astype(jnp.int32) + 1
        ints = jnp.round(piece * (LEVELS / scale_of(level))).astype(jnp.int32)
        return ints[:half] * 65536 + ints[half:], level

    def unpack(words, level, weight):
        high = (words + 32768) >> 16
        low = words - high * 65536
        scale = scale_of(level) * (weight * (1.0 / LEVELS))
        return high.astype(jnp.float32) * scale, low.astype(jnp.float32) * scale

    x_copies = [[] for _ in range(CH)]
    total = jnp.zeros((1, CW), jnp.float32)
    for k in range(CH):
        for copy in g_copies[k]:
            copy.wait_recv()
        cols = slice(k * CW, (k + 1) * CW)
        for h in range(2):
            block = lax.dot_general(
                a_perm[:, h * 4 * XR:(h + 1) * 4 * XR], g_all[:, cols], (((0,), (0,)), ((), ())),
                preferred_element_type=jnp.float32)
            total = total + jnp.sum(block * block, axis=0, keepdims=True)
            if h == 1:
                own_part[:, cols] = block[3 * XR:]
            for t in range(4 - h):
                words, level = pack(block[t * XR:(t + 1) * XR])
                n = h * 4 + t
                x_out[k, n, 0:XR // 2, :] = words
                x_out[k, n, XR // 2:, :] = jnp.broadcast_to(level, (8, CW))
                copy = pltpu.make_async_remote_copy(
                    src_ref=x_out.at[k, n], dst_ref=x_in.at[k, n],
                    send_sem=x_send.at[k, n], recv_sem=x_recv.at[k, n], device_id=in_group(*GROUP[n]), device_id_type=MESH)
                copy.start()
                x_copies[k].append(copy)

    pl.semaphore_wait(met.at[2], 2)

    square = jnp.sum(total, axis=1, keepdims=True)
    row = lax.broadcasted_iota(jnp.int32, (8, 128), 0)
    stat = jnp.where(row < 4, jnp.broadcast_to(square, (8, 128)), jnp.broadcast_to(mask, (8, 128)))
    stat_out[...] = stat
    s_copies = []
    for i, (dy, dc) in enumerate(aug_peers):
        copy = pltpu.make_async_remote_copy(
            src_ref=stat_out, dst_ref=stat_in.at[i], send_sem=s_send.at[i], recv_sem=s_recv.at[i],
            device_id=at_y(dy, dc), device_id_type=MESH)
        copy.start()
        s_copies.append(copy)
    for copy in s_copies:
        copy.wait_recv()
    near = (stat + stat_in[0]) + (stat_in[3] + stat_in[4])
    far = (stat_in[1] + stat_in[2]) + (stat_in[5] + stat_in[6])
    stat = near + far
    count = stat[4:5, :]
    norm = jnp.sqrt(stat[0:1, :]) / count
    factor = CLIP / jnp.maximum(norm, CLIP)
    weight = factor / count
    norm_ref[...] = norm[:, 0:1]
    fac_out[...] = jnp.broadcast_to(weight, (8, 128))
    f_copies = []
    for n in range(7):
        copy = pltpu.make_async_remote_copy(
            src_ref=fac_out, dst_ref=fac_in.at[n], send_sem=f_send.at[n], recv_sem=f_recv.at[n],
            device_id=in_group(*GROUP[n]), device_id_type=MESH)
        copy.start()
        f_copies.append(copy)

    for copy in f_copies:
        copy.wait_recv()
    half = XR // 2
    for k in range(CH):
        cols = slice(k * CW, (k + 1) * CW)
        high, low = weight * own_part[0:half, cols], weight * own_part[half:, cols]
        for n in range(7):
            x_copies[k][n].wait_recv()
            one, two = unpack(x_in[k, n, 0:half, :], x_in[k, n, half:half + 1, :], fac_in[n, 0:1, :])
            high = high + one
            low = low + two
        parts[0:half, cols] = high
        parts[half:, cols] = low

    z_copies = []
    for d in Z_ORDER:
        words, level = pack(parts[d * ZR:(d + 1) * ZR, :])
        if d == 0:
            own_ref[0:6, :], own_ref[6:12, :] = unpack(words, level, 1.0)
            continue
        z_out[d - 1, 0:6, :] = words
        z_out[d - 1, 6:8, :] = jnp.broadcast_to(level, (2, BW))
        copy = pltpu.make_async_remote_copy(
            src_ref=z_out.at[d - 1], dst_ref=z_in.at[d - 1], send_sem=z_send.at[d - 1], recv_sem=z_recv.at[d - 1],
            device_id=at_z(2 * d), device_id_type=MESH)
        copy.start()
        z_copies.append((d, copy))

    top_rows = low_rows = None
    for d, copy in reversed(z_copies):
        copy.wait_recv()
        words = z_in[d - 1]
        one, two = unpack(words[0:6], words[6:7], 1.0)
        top_rows = one if top_rows is None else top_rows + one
        low_rows = two if low_rows is None else low_rows + two
    rest_ref[0:6, :] = top_rows
    rest_ref[6:12, :] = low_rows

    for copy in a_copies + sum(g_copies, []) + sum(x_copies, []) + s_copies + f_copies + [copy for _, copy in z_copies]:
        copy.wait_send()


def per_device(activations, out_grads, kept_mask, noise_field):
    vmem = pl.BlockSpec(memory_space=pltpu.VMEM)
    hbm = pl.BlockSpec(memory_space=pl.ANY)
    dma = pltpu.SemaphoreType.DMA
    bf16, f32, i32 = jnp.bfloat16, jnp.float32, jnp.int32
    own, rest, norm = pl.pallas_call(
        kernel,
        out_shape=(
            jax.ShapeDtypeStruct((ZR, BW), f32), jax.ShapeDtypeStruct((ZR, BW), f32), jax.ShapeDtypeStruct((1, 1), f32)),
        in_specs=[hbm, hbm, vmem],
        out_specs=(vmem,) * 3,
        scratch_shapes=[
            pltpu.VMEM((S, D), bf16),
            pltpu.VMEM((S, FF), bf16),
            pltpu.VMEM((8 * SP, D), bf16),
            pltpu.VMEM((8 * SP, D), bf16),
            pltpu.VMEM((SP, FF), bf16),
            pltpu.VMEM((8 * SP, BW), bf16),
            pltpu.VMEM((D, D), bf16),
            pltpu.VMEM((XR, BW), f32),
            pltpu.VMEM((CH, 7, XR // 2 + 8, CW), i32),
            pltpu.VMEM((CH, 7, XR // 2 + 8, CW), i32),
            pltpu.VMEM((XR, BW), f32),
            pltpu.VMEM((8, 128), f32),
            pltpu.VMEM((7, 8, 128), f32),
            pltpu.VMEM((8, 128), f32),
            pltpu.VMEM((7, 8, 128), f32),
            pltpu.VMEM((7, 8, BW), i32),
            pltpu.VMEM((7, 8, BW), i32),
            dma((2,)), dma((10,)), dma((10,)), dma((CH, 7)), dma((CH, 7)), dma((CH, 7)), dma((CH, 7)),
            dma((7,)), dma((7,)), dma((7,)), dma((7,)), dma((7,)), dma((7,)), dma, pltpu.SemaphoreType.REGULAR((3,)),
        ],
        compiler_params=pltpu.CompilerParams(collective_id=0, has_side_effects=True, vmem_limit_bytes=56 * 2**20),
        name="clipped_sum",
    )(activations[0, 0], out_grads[0, 0], kept_mask)
    clipped = own + rest
    update = (clipped + CLIP * noise_field) * (1.0 / IMAGES)
    return clipped, update, norm.reshape(1)


def solution(mesh):
    in_specs = (
        P("img", "aug", None, None),
        P("img", "aug", None, None),
        P("img", "aug"),
        P("img", "aug"),
    )
    out_specs = (P("img", "aug"), P("img", "aug"), P("img"))
    return jax.shard_map(
        per_device, mesh=mesh, in_specs=in_specs, out_specs=out_specs, check_vma=False
    )
```

```python
import functools
import math

import jax
import jax.numpy as jnp
from jax import lax
from jax.experimental import pallas as pl
from jax.experimental.pallas import tpu as pltpu
from jax.sharding import PartitionSpec as P

MESH = pl.DeviceIdType.MESH
NZ, NX, NY = 16, 4, 4
S, D, FF = 197, 768, 3072
SP = 208
BW = FF // 8
CH = 3
CW = BW // CH
XR = D // 8
ZR = D // (NX * NZ)
IMAGES = 64
CLIP = 0.01 * math.sqrt(D * FF * S)
LEVELS = 32766.0
GROUP = ((2, 1), (2, 0), (1, 1), (1, 0), (3, 1), (3, 0), (0, 1), (0, 0))
Z_ORDER = (4, 3, 5, 2, 6, 1, 7, 0)


def kernel(
    a_hbm, g_hbm, m_ref,
    own_ref, rest_ref, norm_ref,
    a_raw, g_raw, a_all, a_perm, g_pad, g_all, perm, half_sum, p_out, p_in, own_part, x_out, x_in, parts,
    stat_out, stat_in, fac_out, fac_in, z_out, z_in,
    in_sem, a_send, a_recv, g_send, g_recv, p_send, p_recv, x_send, x_recv, s_send, s_recv, f_send, f_recv, z_send, z_recv, own_sem, met,
):
    img, aug = lax.axis_index("img"), lax.axis_index("aug")
    z, x, y, c = img // NX, lax.rem(img, NX), aug // 2, lax.rem(aug, 2)

    mate = (1 - 2 * lax.rem(y, 2)) * (1 - 2 * c)

    def at_y(dy, dc):
        return (img, lax.rem(y + dy + NY, NY) * 2 + (lax.rem(c + dc, 2)))

    def block_of(dy, dc):
        return lax.rem(y + dy + NY, NY) * 2 + lax.rem(c + dc, 2)

    pair = z + 1 - 2 * lax.rem(z, 2)

    def in_group(dx, other):
        return ((pair if other else z) * NX + lax.rem(x + dx, NX), aug)

    def at_z(dz):
        return (lax.rem(z + dz + NZ, NZ) * NX + x, aug)

    partners = (
        (2, (mate, 0), ((2, 0), (mate, 0))),
        (3, (-mate, 1), ((2, 1), (-mate, 1))),
        (1, (0, 1), ((mate, 1), (0, 1))),
    )
    aug_peers = [(dy, dc) for dy in range(NY) for dc in range(2) if (dy, dc) != (0, 0)]

    barrier = pltpu.get_barrier_semaphore()
    for dy, dc in aug_peers:
        pl.semaphore_signal(barrier, inc=1, device_id=at_y(dy, dc), device_id_type=MESH)
    for dx, other in GROUP[:7]:
        pl.semaphore_signal(barrier, inc=1, device_id=in_group(dx, other), device_id_type=MESH)
    pl.semaphore_signal(barrier, inc=1, device_id=at_z(1 - 2 * lax.rem(z + 1, 2)), device_id_type=MESH)

    a_load = pltpu.make_async_copy(a_hbm, a_raw, in_sem.at[0])
    g_load = pltpu.make_async_copy(g_hbm, g_raw, in_sem.at[1])
    a_load.start()
    g_load.start()

    mask = m_ref[...].astype(jnp.float32)
    a_load.wait()
    a_all[0:192, :] = (a_raw[0:192, :].astype(jnp.float32) * mask).astype(jnp.bfloat16)
    a_all[192:SP, :] = jnp.zeros((SP - 192, D), jnp.bfloat16)
    a_all[192:S, :] = (a_raw[192:S, :].astype(jnp.float32) * mask).astype(jnp.bfloat16)

    pl.semaphore_wait(barrier, 7 + 7 + 1)

    def call_z(step):
        for dz in (1 << step, -(1 << step)):
            pl.semaphore_signal(met.at[step], inc=1, device_id=at_z(dz), device_id_type=MESH)

    call_z(0)

    a_copies = []
    for slot, device, _ in partners:
        copy = pltpu.make_async_remote_copy(
            src_ref=a_all.at[pl.ds(0, SP)], dst_ref=a_all.at[pl.ds(slot * SP, SP)],
            send_sem=a_send.at[slot - 1], recv_sem=a_recv.at[slot - 1], device_id=at_y(*device), device_id_type=MESH)
        copy.start()
        a_copies.append(copy)

    pl.semaphore_wait(met.at[0], 2)
    call_z(1)
    g_load.wait()
    g_pad[0:192, :] = g_raw[0:192, :]
    g_pad[192:SP, :] = jnp.zeros((SP - 192, FF), jnp.bfloat16)
    g_pad[192:S, :] = g_raw[192:S, :]
    def columns(block, k, width):
        return pl.ds(pl.multiple_of(block * BW + k * CW, CW), width)

    own_copies = []
    for b, block in enumerate((block_of(-mate, 0), block_of(0, 0))):
        copy = pltpu.make_async_copy(g_pad.at[:, columns(block, 0, BW)], g_all.at[b, pl.ds(0, SP)], own_sem.at[b])
        copy.start()
        own_copies.append(copy)
    g_copies = {}
    for b in range(2):
        for k in range(CH):
            g_copies[b, k] = []
            for slot, device, blocks in partners:
                copy = pltpu.make_async_remote_copy(
                    src_ref=g_pad.at[:, columns(block_of(*blocks[b]), k, CW)],
                    dst_ref=g_all.at[b, pl.ds(slot * SP, SP), pl.ds(k * CW, CW)],
                    send_sem=g_send.at[b, k, slot - 1], recv_sem=g_recv.at[b, k, slot - 1],
                    device_id=at_y(*device), device_id_type=MESH)
                copy.start()
                g_copies[b, k].append(copy)

    pl.semaphore_wait(met.at[1], 2)
    call_z(2)

    p = lax.broadcasted_iota(jnp.int32, (1, D), 1)
    pn, pj, pr = p // XR, lax.rem(p, XR) // ZR, lax.rem(p, ZR)
    step_x = jnp.where(pn < 2, 2, jnp.where(pn < 4, 1, jnp.where(pn < 6, 3, 0)))
    from_z = jnp.where(lax.rem(pn, 2) == 0, pair, z)
    source = lax.rem(from_z + 2 * pj, NZ) * (NX * ZR) + lax.rem(x + step_x, NX) * ZR + pr
    perm[...] = (lax.broadcasted_iota(jnp.int32, (D, D), 0) == source).astype(jnp.bfloat16)

    def permute(s):
        rows = slice(s * SP, (s + 1) * SP)
        a_perm[rows, :] = jnp.dot(a_all[rows, :], perm[...], preferred_element_type=jnp.float32).astype(jnp.bfloat16)

    permute(0)
    for copy, slot in zip(reversed(a_copies), (1, 3, 2)):
        copy.wait_recv()
        permute(slot)
    for copy in own_copies:
        copy.wait()

    def scale_of(level):
        return jnp.exp2(level.astype(jnp.float32) * (1.0 / 64.0))

    def pack(piece):
        half = piece.shape[0] // 2
        top = jnp.maximum(jnp.max(jnp.abs(piece), axis=0, keepdims=True), 1e-30)
        level = jnp.ceil(jnp.log2(top) * 64.0).astype(jnp.int32) + 1
        ints = jnp.round(piece * (LEVELS / scale_of(level))).astype(jnp.int32)
        return ints[:half] * 65536 + ints[half:], level

    def unpack(words, level, weight):
        high = (words + 32768) >> 16
        low = words - high * 65536
        scale = scale_of(level) * (weight * (1.0 / LEVELS))
        return high.astype(jnp.float32) * scale, low.astype(jnp.float32) * scale

    half = D // 2
    p_copies = {}
    for b in range(2):
        for k in range(CH):
            for copy in g_copies[b, k]:
                copy.wait_recv()
            cols = slice(k * CW, (k + 1) * CW)
            for h in range(2):
                block = lax.dot_general(
                    a_perm[:, h * half:(h + 1) * half], g_all[b, :, cols], (((0,), (0,)), ((), ())),
                    preferred_element_type=jnp.float32)
                if b:
                    half_sum[h * half:(h + 1) * half, cols] = block
                    continue
                words, level = pack(block)
                p_out[k, h, 0:half // 2, :] = words
                p_out[k, h, half // 2:, :] = jnp.broadcast_to(level, (8, CW))
                copy = pltpu.make_async_remote_copy(
                    src_ref=p_out.at[k, h], dst_ref=p_in.at[k, h],
                    send_sem=p_send.at[k, h], recv_sem=p_recv.at[k, h], device_id=at_y(-mate, 0), device_id_type=MESH)
                copy.start()
                p_copies[k, h] = copy
    for copy in a_copies + sum(g_copies.values(), []):
        copy.wait_send()

    x_copies = [[] for _ in range(CH)]
    total = jnp.zeros((1, CW), jnp.float32)
    for k in range(CH):
        cols = slice(k * CW, (k + 1) * CW)
        for h in range(2):
            p_copies[k, h].wait_recv()
            parts_of = unpack(p_in[k, h, 0:half // 2, :], p_in[k, h, half // 2:half // 2 + 1, :], 1.0)
            block = jnp.concatenate(parts_of, axis=0) + half_sum[h * half:(h + 1) * half, cols]
            total = total + jnp.sum(block * block, axis=0, keepdims=True)
            if h == 1:
                own_part[:, cols] = block[3 * XR:]
            for t in range(4 - h):
                words, level = pack(block[t * XR:(t + 1) * XR])
                n = h * 4 + t
                x_out[k, n, 0:XR // 2, :] = words
                x_out[k, n, XR // 2:, :] = jnp.broadcast_to(level, (8, CW))
                copy = pltpu.make_async_remote_copy(
                    src_ref=x_out.at[k, n], dst_ref=x_in.at[k, n],
                    send_sem=x_send.at[k, n], recv_sem=x_recv.at[k, n], device_id=in_group(*GROUP[n]), device_id_type=MESH)
                copy.start()
                x_copies[k].append(copy)

    pl.semaphore_wait(met.at[2], 2)

    square = jnp.sum(total, axis=1, keepdims=True)
    row = lax.broadcasted_iota(jnp.int32, (8, 128), 0)
    stat = jnp.where(row < 4, jnp.broadcast_to(square, (8, 128)), jnp.broadcast_to(mask, (8, 128)))
    stat_out[...] = stat
    s_copies = []
    for i, (dy, dc) in enumerate(aug_peers):
        copy = pltpu.make_async_remote_copy(
            src_ref=stat_out, dst_ref=stat_in.at[i], send_sem=s_send.at[i], recv_sem=s_recv.at[i],
            device_id=at_y(dy, dc), device_id_type=MESH)
        copy.start()
        s_copies.append(copy)
    for copy in s_copies:
        copy.wait_recv()
    near = (stat + stat_in[0]) + (stat_in[3] + stat_in[4])
    far = (stat_in[1] + stat_in[2]) + (stat_in[5] + stat_in[6])
    stat = near + far
    count = stat[4:5, :]
    norm = jnp.sqrt(stat[0:1, :]) / count
    factor = CLIP / jnp.maximum(norm, CLIP)
    weight = factor / count
    norm_ref[...] = norm[:, 0:1]
    fac_out[...] = jnp.broadcast_to(weight, (8, 128))
    f_copies = []
    for n in range(7):
        copy = pltpu.make_async_remote_copy(
            src_ref=fac_out, dst_ref=fac_in.at[n], send_sem=f_send.at[n], recv_sem=f_recv.at[n],
            device_id=in_group(*GROUP[n]), device_id_type=MESH)
        copy.start()
        f_copies.append(copy)

    for copy in f_copies:
        copy.wait_recv()
    half = XR // 2
    for k in range(CH):
        cols = slice(k * CW, (k + 1) * CW)
        high, low = weight * own_part[0:half, cols], weight * own_part[half:, cols]
        for n in range(7):
            x_copies[k][n].wait_recv()
            one, two = unpack(x_in[k, n, 0:half, :], x_in[k, n, half:half + 1, :], fac_in[n, 0:1, :])
            high = high + one
            low = low + two
        parts[0:half, cols] = high
        parts[half:, cols] = low

    z_copies = []
    for d in Z_ORDER:
        words, level = pack(parts[d * ZR:(d + 1) * ZR, :])
        if d == 0:
            own_ref[0:6, :], own_ref[6:12, :] = unpack(words, level, 1.0)
            continue
        z_out[d - 1, 0:6, :] = words
        z_out[d - 1, 6:8, :] = jnp.broadcast_to(level, (2, BW))
        copy = pltpu.make_async_remote_copy(
            src_ref=z_out.at[d - 1], dst_ref=z_in.at[d - 1], send_sem=z_send.at[d - 1], recv_sem=z_recv.at[d - 1],
            device_id=at_z(2 * d), device_id_type=MESH)
        copy.start()
        z_copies.append((d, copy))

    for copy in list(p_copies.values()) + sum(x_copies, []) + s_copies + f_copies:
        copy.wait_send()
    top_rows = low_rows = None
    for d, copy in reversed(z_copies):
        copy.wait_recv()
        words = z_in[d - 1]
        one, two = unpack(words[0:6], words[6:7], 1.0)
        top_rows = one if top_rows is None else top_rows + one
        low_rows = two if low_rows is None else low_rows + two
    rest_ref[0:6, :] = top_rows
    rest_ref[6:12, :] = low_rows

    for _, copy in z_copies:
        copy.wait_send()


def per_device(activations, out_grads, kept_mask, noise_field):
    vmem = pl.BlockSpec(memory_space=pltpu.VMEM)
    hbm = pl.BlockSpec(memory_space=pl.ANY)
    dma = pltpu.SemaphoreType.DMA
    bf16, f32, i32 = jnp.bfloat16, jnp.float32, jnp.int32
    own, rest, norm = pl.pallas_call(
        kernel,
        out_shape=(
            jax.ShapeDtypeStruct((ZR, BW), f32), jax.ShapeDtypeStruct((ZR, BW), f32), jax.ShapeDtypeStruct((1, 1), f32)),
        in_specs=[hbm, hbm, vmem],
        out_specs=(vmem,) * 3,
        scratch_shapes=[
            pltpu.VMEM((S, D), bf16),
            pltpu.VMEM((S, FF), bf16),
            pltpu.VMEM((4 * SP, D), bf16),
            pltpu.VMEM((4 * SP, D), bf16),
            pltpu.VMEM((SP, FF), bf16),
            pltpu.VMEM((2, 4 * SP, BW), bf16),
            pltpu.VMEM((D, D), bf16),
            pltpu.VMEM((D, BW), f32),
            pltpu.VMEM((CH, 2, D // 4 + 8, CW), i32),
            pltpu.VMEM((CH, 2, D // 4 + 8, CW), i32),
            pltpu.VMEM((XR, BW), f32),
            pltpu.VMEM((CH, 7, XR // 2 + 8, CW), i32),
            pltpu.VMEM((CH, 7, XR // 2 + 8, CW), i32),
            pltpu.VMEM((XR, BW), f32),
            pltpu.VMEM((8, 128), f32),
            pltpu.VMEM((7, 8, 128), f32),
            pltpu.VMEM((8, 128), f32),
            pltpu.VMEM((7, 8, 128), f32),
            pltpu.VMEM((7, 8, BW), i32),
            pltpu.VMEM((7, 8, BW), i32),
            dma((2,)), dma((3,)), dma((3,)), dma((2, CH, 3)), dma((2, CH, 3)), dma((CH, 2)), dma((CH, 2)), dma((CH, 7)), dma((CH, 7)),
            dma((7,)), dma((7,)), dma((7,)), dma((7,)), dma((7,)), dma((7,)), dma((2,)), pltpu.SemaphoreType.REGULAR((3,)),
        ],
        compiler_params=pltpu.CompilerParams(collective_id=0, has_side_effects=True, vmem_limit_bytes=53 * 2**20 + 700000),
        name="clipped_sum",
    )(activations[0, 0], out_grads[0, 0], kept_mask)
    clipped = own + rest
    update = (clipped + CLIP * noise_field) * (1.0 / IMAGES)
    return clipped, update, norm.reshape(1)


def solution(mesh):
    in_specs = (
        P("img", "aug", None, None),
        P("img", "aug", None, None),
        P("img", "aug"),
        P("img", "aug"),
    )
    out_specs = (P("img", "aug"), P("img", "aug"), P("img"))
    return jax.shard_map(
        per_device, mesh=mesh, in_specs=in_specs, out_specs=out_specs, check_vma=False
    )
```

```python
import functools
import math

import jax
import jax.numpy as jnp
from jax import lax
from jax.experimental import pallas as pl
from jax.experimental.pallas import tpu as pltpu
from jax.sharding import PartitionSpec as P

MESH = pl.DeviceIdType.MESH
NZ, NX, NY = 16, 4, 4
S, D, FF = 197, 768, 3072
SP = 208
BW = FF // 8
CH = 3
CW = BW // CH
XR = D // 8
ZR = D // (NX * NZ)
IMAGES = 64
CLIP = 0.01 * math.sqrt(D * FF * S)
LEVELS = 32766.0
GROUP = ((2, 1), (2, 0), (1, 1), (1, 0), (3, 1), (3, 0), (0, 1), (0, 0))
Z_ORDER = (4, 3, 5, 2, 6, 1, 7, 0)


def kernel(
    a_hbm, g_hbm, m_ref,
    own_ref, rest_ref, norm_ref,
    a_raw, g_raw, a_all, a_perm, g_pad, g_all, perm, half_sum, p_out, p_in, own_part, x_out, x_in, x_part, parts,
    stat_out, stat_in, fac_out, fac_in, z_out, z_in,
    in_sem, a_send, a_recv, g_send, g_recv, p_send, p_recv, x_send, x_recv, s_send, s_recv, f_send, f_recv, z_send, z_recv, own_sem, met,
):
    img, aug = lax.axis_index("img"), lax.axis_index("aug")
    z, x, y, c = img // NX, lax.rem(img, NX), aug // 2, lax.rem(aug, 2)

    mate = (1 - 2 * lax.rem(y, 2)) * (1 - 2 * c)

    def at_y(dy, dc):
        return (img, lax.rem(y + dy + NY, NY) * 2 + (lax.rem(c + dc, 2)))

    def block_of(dy, dc):
        return lax.rem(y + dy + NY, NY) * 2 + lax.rem(c + dc, 2)

    pair = z + 1 - 2 * lax.rem(z, 2)

    def in_group(dx, other):
        return ((pair if other else z) * NX + lax.rem(x + dx, NX), aug)

    def at_z(dz):
        return (lax.rem(z + dz + NZ, NZ) * NX + x, aug)

    partners = (
        (2, (mate, 0), ((2, 0), (mate, 0))),
        (3, (-mate, 1), ((2, 1), (-mate, 1))),
        (1, (0, 1), ((mate, 1), (0, 1))),
    )
    aug_peers = [(dy, dc) for dy in range(NY) for dc in range(2) if (dy, dc) != (0, 0)]

    barrier = pltpu.get_barrier_semaphore()
    next_to = [at_y(0, 1), at_y(1, 0), at_y(1, 1), at_y(-1, 0), at_y(-1, 1)]
    next_to += [in_group(1, 0), in_group(NX - 1, 0), at_z(1), at_z(-1)]
    for device in next_to:
        pl.semaphore_signal(barrier, inc=1, device_id=device, device_id_type=MESH)

    a_load = pltpu.make_async_copy(a_hbm, a_raw, in_sem.at[0])
    g_load = pltpu.make_async_copy(g_hbm, g_raw, in_sem.at[1])
    a_load.start()
    g_load.start()

    mask = m_ref[...].astype(jnp.float32)
    a_load.wait()
    a_all[0:192, :] = (a_raw[0:192, :].astype(jnp.float32) * mask).astype(jnp.bfloat16)
    a_all[192:SP, :] = jnp.zeros((SP - 192, D), jnp.bfloat16)
    a_all[192:S, :] = (a_raw[192:S, :].astype(jnp.float32) * mask).astype(jnp.bfloat16)

    pl.semaphore_wait(barrier, 9)

    def call(step, devices):
        for device in devices:
            pl.semaphore_signal(met.at[step], inc=1, device_id=device, device_id_type=MESH)

    call(0, [at_y(1, 0), in_group(1, 0), in_group(NX - 1, 0), at_z(1), at_z(-1)])

    def whole(ref, sem):
        pltpu.make_async_copy(ref, ref, sem).wait()

    a_copies = []
    for slot, device, _ in partners:
        copy = pltpu.make_async_remote_copy(
            src_ref=a_all.at[pl.ds(0, SP)], dst_ref=a_all.at[pl.ds(slot * SP, SP)],
            send_sem=a_send, recv_sem=a_recv.at[slot - 1], device_id=at_y(*device), device_id_type=MESH)
        copy.start()
        a_copies.append(copy)

    pl.semaphore_wait(met.at[0], 5)
    call(1, [in_group(1, 0), at_z(2), at_z(-2)])
    g_load.wait()
    g_pad[0:192, :] = g_raw[0:192, :]
    g_pad[192:SP, :] = jnp.zeros((SP - 192, FF), jnp.bfloat16)
    g_pad[192:S, :] = g_raw[192:S, :]
    def columns(block, k, width):
        return pl.ds(pl.multiple_of(block * BW + k * CW, CW), width)

    for b, block in enumerate((block_of(-mate, 0), block_of(0, 0))):
        copy = pltpu.make_async_copy(g_pad.at[:, columns(block, 0, BW)], g_all.at[b, pl.ds(0, SP)], own_sem)
        copy.start()
    for b in range(2):
        for k in range(CH):
            for slot, device, blocks in partners:
                copy = pltpu.make_async_remote_copy(
                    src_ref=g_pad.at[:, columns(block_of(*blocks[b]), k, CW)],
                    dst_ref=g_all.at[b, pl.ds(slot * SP, SP), pl.ds(k * CW, CW)],
                    send_sem=g_send, recv_sem=g_recv.at[b, k],
                    device_id=at_y(*device), device_id_type=MESH)
                copy.start()

    pl.semaphore_wait(met.at[1], 3)
    call(2, [at_z(4), at_z(-4)])

    p = lax.broadcasted_iota(jnp.int32, (1, D), 1)
    pn, pj, pr = p // XR, lax.rem(p, XR) // ZR, lax.rem(p, ZR)
    step_x = jnp.where(pn < 2, 2, jnp.where(pn < 4, 1, jnp.where(pn < 6, 3, 0)))
    from_z = jnp.where(lax.rem(pn, 2) == 0, pair, z)
    source = lax.rem(from_z + 2 * pj, NZ) * (NX * ZR) + lax.rem(x + step_x, NX) * ZR + pr
    perm[...] = (lax.broadcasted_iota(jnp.int32, (D, D), 0) == source).astype(jnp.bfloat16)

    def permute(s):
        rows = slice(s * SP, (s + 1) * SP)
        a_perm[rows, :] = jnp.dot(a_all[rows, :], perm[...], preferred_element_type=jnp.float32).astype(jnp.bfloat16)

    permute(0)
    for copy, slot in zip(reversed(a_copies), (1, 3, 2)):
        copy.wait_recv()
        permute(slot)
    whole(g_all.at[:, pl.ds(0, SP)], own_sem)

    def scale_of(level):
        return jnp.exp2(level.astype(jnp.float32) * (1.0 / 64.0))

    def pack(piece):
        half = piece.shape[0] // 2
        top = jnp.maximum(jnp.max(jnp.abs(piece), axis=0, keepdims=True), 1e-30)
        level = jnp.ceil(jnp.log2(top) * 64.0).astype(jnp.int32) + 1
        ints = jnp.round(piece * (LEVELS / scale_of(level))).astype(jnp.int32)
        return ints[:half] * 65536 + ints[half:], level

    def unpack(words, level, weight):
        high = (words + 32768) >> 16
        low = words - high * 65536
        scale = scale_of(level) * (weight * (1.0 / LEVELS))
        return high.astype(jnp.float32) * scale, low.astype(jnp.float32) * scale

    half = D // 2
    p_copies = {}
    for b in range(2):
        for k in range(CH):
            whole(g_all.at[b, pl.ds(SP, 3 * SP), pl.ds(k * CW, CW)], g_recv.at[b, k])
            cols = slice(k * CW, (k + 1) * CW)
            for h in range(2):
                block = lax.dot_general(
                    a_perm[:, h * half:(h + 1) * half], g_all[b, :, cols], (((0,), (0,)), ((), ())),
                    preferred_element_type=jnp.float32)
                if b:
                    half_sum[h * half:(h + 1) * half, cols] = block
                    continue
                words, level = pack(block)
                p_out[k, h, 0:half // 2, :] = words
                p_out[k, h, half // 2:, :] = level
                copy = pltpu.make_async_remote_copy(
                    src_ref=p_out.at[k, h], dst_ref=p_in.at[k, h],
                    send_sem=p_send, recv_sem=p_recv.at[k, h], device_id=at_y(-mate, 0), device_id_type=MESH)
                copy.start()
                p_copies[k, h] = copy
    whole(a_all.at[pl.ds(SP, 3 * SP)], a_send)
    whole(g_all.at[:, pl.ds(SP, 3 * SP)], g_send)

    total = jnp.zeros((1, CW), jnp.float32)
    for k in range(CH):
        cols = slice(k * CW, (k + 1) * CW)
        for h in range(2):
            p_copies[k, h].wait_recv()
            parts_of = unpack(p_in[k, h, 0:half // 2, :], p_in[k, h, half // 2:half // 2 + 1, :], 1.0)
            block = jnp.concatenate(parts_of, axis=0) + half_sum[h * half:(h + 1) * half, cols]
            total = total + jnp.sum(block * block, axis=0, keepdims=True)
            if (k, h) == (CH - 1, 1):
                square = jnp.sum(total, axis=1, keepdims=True)
                row = lax.broadcasted_iota(jnp.int32, (8, 128), 0)
                stat = jnp.where(row < 4, jnp.broadcast_to(square, (8, 128)), jnp.broadcast_to(mask, (8, 128)))
                stat_out[...] = stat
                for i, (dy, dc) in enumerate(aug_peers):
                    copy = pltpu.make_async_remote_copy(
                        src_ref=stat_out, dst_ref=stat_in.at[i], send_sem=s_send, recv_sem=s_recv,
                        device_id=at_y(dy, dc), device_id_type=MESH)
                    copy.start()
            if h == 1:
                own_part[:, cols] = block[3 * XR:]
            for t in range(4 - h):
                words, level = pack(block[t * XR:(t + 1) * XR])
                n = h * 4 + t
                x_out[k, n, 0:XR // 2, :] = words
                x_out[k, n, XR // 2:, :] = level
                copy = pltpu.make_async_remote_copy(
                    src_ref=x_out.at[k, n], dst_ref=x_in.at[k, n],
                    send_sem=x_send, recv_sem=x_recv.at[k], device_id=in_group(*GROUP[n]), device_id_type=MESH)
                copy.start()

    pl.semaphore_wait(met.at[2], 2)

    whole(stat_in, s_recv)
    near = (stat + stat_in[0]) + (stat_in[3] + stat_in[4])
    far = (stat_in[1] + stat_in[2]) + (stat_in[5] + stat_in[6])
    stat = near + far
    count = stat[4:5, :]
    root = jnp.sqrt(stat[0:1, :])
    weight = CLIP / jnp.maximum(root, CLIP * count)
    fac_out[...] = jnp.broadcast_to(weight, (8, 128))
    for n in range(7):
        copy = pltpu.make_async_remote_copy(
            src_ref=fac_out, dst_ref=fac_in.at[n], send_sem=f_send, recv_sem=f_recv,
            device_id=in_group(*GROUP[n]), device_id_type=MESH)
        copy.start()

    norm_ref[...] = (root / count)[:, 0:1]
    half = XR // 2
    for k in range(CH):
        cols = slice(k * CW, (k + 1) * CW)
        whole(x_in.at[k], x_recv.at[k])
        for n in range(7):
            high, low = unpack(x_in[k, n, 0:half, :], x_in[k, n, half:half + 1, :], 1.0)
            x_part[n, 0:half, cols] = high
            x_part[n, half:, cols] = low
    whole(fac_in, f_recv)
    for k in range(CH):
        cols = slice(k * CW, (k + 1) * CW)
        part = weight * own_part[:, cols]
        for n in range(7):
            part = part + fac_in[n, 0:1, :] * x_part[n, :, cols]
        parts[:, cols] = part

    z_copies = []
    for d in Z_ORDER:
        words, level = pack(parts[d * ZR:(d + 1) * ZR, :])
        if d == 0:
            own_ref[0:6, :], own_ref[6:12, :] = unpack(words, level, 1.0)
            continue
        z_out[d - 1, 0:6, :] = words
        z_out[d - 1, 6:7, :] = level
        copy = pltpu.make_async_remote_copy(
            src_ref=z_out.at[d - 1], dst_ref=z_in.at[d - 1], send_sem=z_send, recv_sem=z_recv.at[d - 1],
            device_id=at_z(2 * d), device_id_type=MESH)
        copy.start()
        z_copies.append((d, copy))

    whole(p_out, p_send)
    whole(x_out, x_send)
    whole(stat_in, s_send)
    whole(fac_in, f_send)
    top_rows = low_rows = None
    for d, copy in reversed(z_copies):
        copy.wait_recv()
        words = z_in[d - 1]
        one, two = unpack(words[0:6], words[6:7], 1.0)
        top_rows = one if top_rows is None else top_rows + one
        low_rows = two if low_rows is None else low_rows + two
    rest_ref[0:6, :] = top_rows
    rest_ref[6:12, :] = low_rows

    whole(z_out, z_send)


def per_device(activations, out_grads, kept_mask, noise_field):
    vmem = pl.BlockSpec(memory_space=pltpu.VMEM)
    hbm = pl.BlockSpec(memory_space=pl.ANY)
    dma = pltpu.SemaphoreType.DMA
    bf16, f32, i32 = jnp.bfloat16, jnp.float32, jnp.int32
    own, rest, norm = pl.pallas_call(
        kernel,
        out_shape=(
            jax.ShapeDtypeStruct((ZR, BW), f32), jax.ShapeDtypeStruct((ZR, BW), f32), jax.ShapeDtypeStruct((1, 1), f32)),
        in_specs=[hbm, hbm, vmem],
        out_specs=(vmem,) * 3,
        scratch_shapes=[
            pltpu.VMEM((S, D), bf16),
            pltpu.VMEM((S, FF), bf16),
            pltpu.VMEM((4 * SP, D), bf16),
            pltpu.VMEM((4 * SP, D), bf16),
            pltpu.VMEM((SP, FF), bf16),
            pltpu.VMEM((2, 4 * SP, BW), bf16),
            pltpu.VMEM((D, D), bf16),
            pltpu.VMEM((D, BW), f32),
            pltpu.VMEM((CH, 2, D // 4 + 1, CW), i32),
            pltpu.VMEM((CH, 2, D // 4 + 1, CW), i32),
            pltpu.VMEM((XR, BW), f32),
            pltpu.VMEM((CH, 7, XR // 2 + 1, CW), i32),
            pltpu.VMEM((CH, 7, XR // 2 + 1, CW), i32),
            pltpu.VMEM((7, XR, BW), f32),
            pltpu.VMEM((XR, BW), f32),
            pltpu.VMEM((8, 128), f32),
            pltpu.VMEM((7, 8, 128), f32),
            pltpu.VMEM((8, 128), f32),
            pltpu.VMEM((7, 8, 128), f32),
            pltpu.VMEM((7, 7, BW), i32),
            pltpu.VMEM((7, 7, BW), i32),
            dma((2,)), dma, dma((3,)), dma, dma((2, CH)), dma, dma((CH, 2)), dma, dma((CH,)),
            dma, dma, dma, dma, dma, dma((7,)), dma, pltpu.SemaphoreType.REGULAR((3,)),
        ],
        compiler_params=pltpu.CompilerParams(collective_id=0, has_side_effects=True, vmem_limit_bytes=53 * 2**20 + 700000),
        name="clipped_sum",
    )(activations[0, 0], out_grads[0, 0], kept_mask)
    clipped = own + rest
    update = (clipped + CLIP * noise_field) * (1.0 / IMAGES)
    return clipped, update, norm.reshape(1)


def solution(mesh):
    in_specs = (
        P("img", "aug", None, None),
        P("img", "aug", None, None),
        P("img", "aug"),
        P("img", "aug"),
    )
    out_specs = (P("img", "aug"), P("img", "aug"), P("img"))
    return jax.shard_map(
        per_device, mesh=mesh, in_specs=in_specs, out_specs=out_specs, check_vma=False
    )
```

```python
import functools
import math

import jax
import jax.numpy as jnp
from jax import lax
from jax.experimental import pallas as pl
from jax.experimental.pallas import tpu as pltpu
from jax.sharding import PartitionSpec as P

MESH = pl.DeviceIdType.MESH
NZ, NX, NY = 16, 4, 4
S, D, FF = 197, 768, 3072
SP = 208
MAIN = 192
BW = FF // 8
CH = 3
CW = BW // CH
XR = D // 8
ZR = D // (NX * NZ)
IMAGES = 64
CLIP = 0.01 * math.sqrt(D * FF * S)
LEVELS = 32766.0
GROUP = ((2, 1), (2, 0), (1, 1), (1, 0), (3, 1), (3, 0), (0, 1), (0, 0))
Z_ORDER = (4, 3, 5, 2, 6, 1, 7, 0)


def kernel(
    a_hbm, g_hbm, m_hbm,
    own_ref, rest_ref,
    a_raw, g_raw, m_ref, tail32, tail_out, tail_in, a_all, a_perm, g_all, perm, half_sum, p_out, p_in, own_part, x_out, x_in, x_part, parts,
    stat_out, stat_in, fac_out, fac_in, z_out, z_in,
    in_sem, t_send, t_recv, a_send, a_recv, g_send, g_recv, p_send, p_recv, x_send, x_recv, s_send, s_recv, f_send, f_recv, z_send, z_recv, met,
):
    img, aug = lax.axis_index("img"), lax.axis_index("aug")
    z, x, y, c = img // NX, lax.rem(img, NX), aug // 2, lax.rem(aug, 2)

    mate = (1 - 2 * lax.rem(y, 2)) * (1 - 2 * c)

    def at_y(dy, dc):
        return (img, lax.rem(y + dy + NY, NY) * 2 + (lax.rem(c + dc, 2)))

    def block_of(dy, dc):
        return lax.rem(y + dy + NY, NY) * 2 + lax.rem(c + dc, 2)

    pair = z + 1 - 2 * lax.rem(z, 2)

    def in_group(dx, other):
        return ((pair if other else z) * NX + lax.rem(x + dx, NX), aug)

    def at_z(dz):
        return (lax.rem(z + dz + NZ, NZ) * NX + x, aug)

    partners = (
        (2, (mate, 0), ((2, 0), (mate, 0))),
        (3, (-mate, 1), ((2, 1), (-mate, 1))),
        (1, (0, 1), ((mate, 1), (0, 1))),
    )
    aug_peers = [(dy, dc) for dy in range(NY) for dc in range(2) if (dy, dc) != (0, 0)]

    barrier = pltpu.get_barrier_semaphore()
    next_to = [at_y(0, 1), at_y(1, 0), at_y(1, 1), at_y(-1, 0), at_y(-1, 1)]
    next_to += [in_group(1, 0), in_group(NX - 1, 0), at_z(1), at_z(-1)]
    for device in next_to:
        pl.semaphore_signal(barrier, inc=1, device_id=device, device_id_type=MESH)

    a_load = pltpu.make_async_copy(a_hbm, a_raw, in_sem.at[0])
    g_load = pltpu.make_async_copy(g_hbm, g_raw, in_sem.at[1])
    m_load = pltpu.make_async_copy(m_hbm, m_ref, in_sem.at[2])
    m_load.start()
    a_load.start()
    g_load.start()

    def columns(block, k, width):
        return pl.ds(pl.multiple_of(block * BW + k * CW, CW), width)

    own_copies = [pltpu.make_async_copy(a_hbm.at[pl.ds(0, MAIN)], a_all.at[0, pl.ds(0, MAIN)], in_sem.at[3])]
    for b, block in enumerate((block_of(-mate, 0), block_of(0, 0))):
        own_copies.append(pltpu.make_async_copy(
            g_hbm.at[pl.ds(0, MAIN), columns(block, 0, BW)], g_all.at[b, 0, pl.ds(0, MAIN)], in_sem.at[4 + b]))
    for copy in own_copies:
        copy.start()

    pl.semaphore_wait(barrier, 9)

    def call(step, devices):
        for device in devices:
            pl.semaphore_signal(met.at[step], inc=1, device_id=device, device_id_type=MESH)

    call(0, [at_y(1, 0), in_group(1, 0), in_group(NX - 1, 0), at_z(1), at_z(-1)])

    def whole(ref, sem):
        pltpu.make_async_copy(ref, ref, sem).wait()

    a_copies = []
    for slot, device, _ in partners:
        copy = pltpu.make_async_remote_copy(
            src_ref=a_hbm.at[pl.ds(0, MAIN)], dst_ref=a_all.at[slot, pl.ds(0, MAIN)],
            send_sem=a_send, recv_sem=a_recv.at[slot - 1], device_id=at_y(*device), device_id_type=MESH)
        copy.start()
        a_copies.append(copy)

    m_load.wait()
    mask = m_ref[...].astype(jnp.float32)
    a_load.wait()
    g_load.wait()
    tail32[...] = jnp.zeros_like(tail32)
    targets = [(0, (), ((-mate, 0), (0, 0)))] + list(partners)
    for i, (slot, device, blocks) in enumerate(targets):
        tail32[i, 0:S - MAIN, :] = a_raw[MAIN:S, :].astype(jnp.float32)
        tail32[i, 5:6, :] = jnp.broadcast_to(mask, (1, D))
        for b in range(2):
            tail32[i, 8:8 + S - MAIN, b * BW:(b + 1) * BW] = g_raw[
                MAIN:S, columns(block_of(*blocks[b]), 0, BW)].astype(jnp.float32)
        if slot == 0:
            tail_in[0] = tail32[i].astype(jnp.bfloat16)
            continue
        tail_out[i - 1] = tail32[i].astype(jnp.bfloat16)
        pltpu.make_async_remote_copy(
            src_ref=tail_out.at[i - 1], dst_ref=tail_in.at[slot], send_sem=t_send, recv_sem=t_recv,
            device_id=at_y(*device), device_id_type=MESH).start()

    for b in range(2):
        for k in range(CH):
            for slot, device, blocks in partners:
                copy = pltpu.make_async_remote_copy(
                    src_ref=g_raw.at[pl.ds(0, MAIN), columns(block_of(*blocks[b]), k, CW)],
                    dst_ref=g_all.at[b, slot, pl.ds(0, MAIN), pl.ds(k * CW, CW)],
                    send_sem=g_send, recv_sem=g_recv.at[b, k],
                    device_id=at_y(*device), device_id_type=MESH)
                copy.start()

    pl.semaphore_wait(met.at[0], 5)
    call(1, [in_group(1, 0), at_z(2), at_z(-2)])
    pl.semaphore_wait(met.at[1], 3)
    call(2, [at_z(4), at_z(-4)])

    p = lax.broadcasted_iota(jnp.int32, (1, D), 1)
    pn, pj, pr = p // XR, lax.rem(p, XR) // ZR, lax.rem(p, ZR)
    step_x = jnp.where(pn < 2, 2, jnp.where(pn < 4, 1, jnp.where(pn < 6, 3, 0)))
    from_z = jnp.where(lax.rem(pn, 2) == 0, pair, z)
    source = lax.rem(from_z + 2 * pj, NZ) * (NX * ZR) + lax.rem(x + step_x, NX) * ZR + pr
    perm[...] = (lax.broadcasted_iota(jnp.int32, (D, D), 0) == source).astype(jnp.bfloat16)

    def permute(s):
        tail = tail_in[s].astype(jnp.float32)
        row = lax.broadcasted_iota(jnp.int32, (16, D), 0)
        a_all[s, MAIN:SP, :] = jnp.where(row < S - MAIN, tail, 0.0).astype(jnp.bfloat16)
        grads = jnp.where(row[0:8] < S - MAIN, tail[8:16], 0.0)
        grads = jnp.concatenate([grads, jnp.zeros((8, D), jnp.float32)], axis=0).astype(jnp.bfloat16)
        for b in range(2):
            g_all[b, s, MAIN:SP, :] = grads[:, b * BW:(b + 1) * BW]
        product = jnp.dot(a_all[s], perm[...], preferred_element_type=jnp.float32)
        a_perm[s * SP:(s + 1) * SP, :] = (product * tail[5:6, :]).astype(jnp.bfloat16)

    for copy in own_copies:
        copy.wait()
    permute(0)
    whole(tail_in.at[pl.ds(1, 3)], t_recv)
    for copy, slot in zip(reversed(a_copies), (1, 3, 2)):
        copy.wait_recv()
        permute(slot)

    def scale_of(level):
        return jnp.exp2(level.astype(jnp.float32) * (1.0 / 64.0))

    def pack(piece):
        half = piece.shape[0] // 2
        top = jnp.maximum(jnp.max(jnp.abs(piece), axis=0, keepdims=True), 1e-30)
        level = jnp.ceil(jnp.log2(top) * 64.0).astype(jnp.int32) + 1
        ints = jnp.round(piece * (LEVELS / scale_of(level))).astype(jnp.int32)
        return ints[:half] * 65536 + ints[half:], level

    def unpack(words, level, weight):
        high = (words + 32768) >> 16
        low = words - high * 65536
        scale = scale_of(level) * (weight * (1.0 / LEVELS))
        return high.astype(jnp.float32) * scale, low.astype(jnp.float32) * scale

    half = D // 2
    p_copies = {}
    for b in range(2):
        for k in range(CH):
            whole(g_all.at[b, pl.ds(1, 3), pl.ds(0, MAIN), pl.ds(k * CW, CW)], g_recv.at[b, k])
            cols = slice(k * CW, (k + 1) * CW)
            for h in range(2):
                block = lax.dot_general(
                    a_perm[:, h * half:(h + 1) * half], g_all[b, :, :, cols].reshape(4 * SP, CW), (((0,), (0,)), ((), ())),
                    preferred_element_type=jnp.float32)
                if b:
                    half_sum[h * half:(h + 1) * half, cols] = block
                    continue
                words, level = pack(block)
                p_out[k, h, 0:half // 2, :] = words
                p_out[k, h, half // 2:, :] = level
                copy = pltpu.make_async_remote_copy(
                    src_ref=p_out.at[k, h], dst_ref=p_in.at[k, h],
                    send_sem=p_send, recv_sem=p_recv.at[k, h], device_id=at_y(-mate, 0), device_id_type=MESH)
                copy.start()
                p_copies[k, h] = copy
    whole(a_all.at[pl.ds(1, 3), pl.ds(0, MAIN)], a_send)
    whole(g_all.at[:, pl.ds(1, 3), pl.ds(0, MAIN)], g_send)
    whole(tail_out, t_send)

    total = jnp.zeros((1, CW), jnp.float32)
    for k in range(CH):
        cols = slice(k * CW, (k + 1) * CW)
        for h in range(2):
            p_copies[k, h].wait_recv()
            parts_of = unpack(p_in[k, h, 0:half // 2, :], p_in[k, h, half // 2:half // 2 + 1, :], 1.0)
            block = jnp.concatenate(parts_of, axis=0) + half_sum[h * half:(h + 1) * half, cols]
            total = total + jnp.sum(block * block, axis=0, keepdims=True)
            if (k, h) == (CH - 1, 1):
                square = jnp.sum(total, axis=1, keepdims=True)
                row = lax.broadcasted_iota(jnp.int32, (8, 128), 0)
                stat = jnp.where(row < 4, jnp.broadcast_to(square, (8, 128)), jnp.broadcast_to(mask, (8, 128)))
                stat_out[...] = stat
                for i, (dy, dc) in enumerate(aug_peers):
                    copy = pltpu.make_async_remote_copy(
                        src_ref=stat_out, dst_ref=stat_in.at[i], send_sem=s_send, recv_sem=s_recv,
                        device_id=at_y(dy, dc), device_id_type=MESH)
                    copy.start()
            if h == 1:
                own_part[:, cols] = block[3 * XR:]
            for t in range(4 - h):
                words, level = pack(block[t * XR:(t + 1) * XR])
                n = h * 4 + t
                x_out[k, n, 0:XR // 2, :] = words
                x_out[k, n, XR // 2:, :] = level
                copy = pltpu.make_async_remote_copy(
                    src_ref=x_out.at[k, n], dst_ref=x_in.at[k, n],
                    send_sem=x_send, recv_sem=x_recv.at[k], device_id=in_group(*GROUP[n]), device_id_type=MESH)
                copy.start()

    pl.semaphore_wait(met.at[2], 2)

    whole(stat_in, s_recv)
    near = (stat + stat_in[0]) + (stat_in[3] + stat_in[4])
    far = (stat_in[1] + stat_in[2]) + (stat_in[5] + stat_in[6])
    stat = near + far
    count = stat[4:5, :]
    root = jnp.sqrt(stat[0:1, :])
    weight = CLIP / jnp.maximum(root, CLIP * count)
    fac_out[...] = jnp.broadcast_to(weight, (8, 128))
    for n in range(7):
        copy = pltpu.make_async_remote_copy(
            src_ref=fac_out, dst_ref=fac_in.at[n], send_sem=f_send, recv_sem=f_recv,
            device_id=in_group(*GROUP[n]), device_id_type=MESH)
        copy.start()

    rest_ref[ZR:ZR + 1, 0:128] = root / count
    half = XR // 2
    for k in range(CH):
        cols = slice(k * CW, (k + 1) * CW)
        whole(x_in.at[k], x_recv.at[k])
        for n in range(7):
            high, low = unpack(x_in[k, n, 0:half, :], x_in[k, n, half:half + 1, :], 1.0)
            x_part[n, 0:half, cols] = high
            x_part[n, half:, cols] = low
    whole(fac_in, f_recv)
    for k in range(CH):
        cols = slice(k * CW, (k + 1) * CW)
        part = weight * own_part[:, cols]
        for n in range(7):
            part = part + fac_in[n, 0:1, :] * x_part[n, :, cols]
        parts[:, cols] = part

    z_copies = []
    for d in Z_ORDER:
        words, level = pack(parts[d * ZR:(d + 1) * ZR, :])
        if d == 0:
            own_ref[0:6, :], own_ref[6:12, :] = unpack(words, level, 1.0)
            continue
        z_out[d - 1, 0:6, :] = words
        z_out[d - 1, 6:7, :] = level
        copy = pltpu.make_async_remote_copy(
            src_ref=z_out.at[d - 1], dst_ref=z_in.at[d - 1], send_sem=z_send, recv_sem=z_recv.at[d - 1],
            device_id=at_z(2 * d), device_id_type=MESH)
        copy.start()
        z_copies.append((d, copy))

    whole(p_out, p_send)
    whole(x_out, x_send)
    whole(stat_in, s_send)
    whole(fac_in, f_send)
    top_rows = low_rows = None
    for d, copy in reversed(z_copies):
        copy.wait_recv()
        words = z_in[d - 1]
        one, two = unpack(words[0:6], words[6:7], 1.0)
        top_rows = one if top_rows is None else top_rows + one
        low_rows = two if low_rows is None else low_rows + two
    rest_ref[0:6, :] = top_rows
    rest_ref[6:12, :] = low_rows

    whole(z_out, z_send)


def per_device(activations, out_grads, kept_mask, noise_field):
    vmem = pl.BlockSpec(memory_space=pltpu.VMEM)
    hbm = pl.BlockSpec(memory_space=pl.ANY)
    dma = pltpu.SemaphoreType.DMA
    bf16, f32, i32 = jnp.bfloat16, jnp.float32, jnp.int32
    own, rest = pl.pallas_call(
        kernel,
        out_shape=(jax.ShapeDtypeStruct((ZR, BW), f32), jax.ShapeDtypeStruct((16, BW), f32)),
        in_specs=[hbm, hbm, hbm],
        out_specs=(vmem,) * 2,
        scratch_shapes=[
            pltpu.VMEM((S, D), bf16),
            pltpu.VMEM((S, FF), bf16),
            pltpu.VMEM((1, 1), i32),
            pltpu.VMEM((4, 16, D), f32),
            pltpu.VMEM((3, 16, D), bf16),
            pltpu.VMEM((4, 16, D), bf16),
            pltpu.VMEM((4, SP, D), bf16),
            pltpu.VMEM((4 * SP, D), bf16),
            pltpu.VMEM((2, 4, SP, BW), bf16),
            pltpu.VMEM((D, D), bf16),
            pltpu.VMEM((D, BW), f32),
            pltpu.VMEM((CH, 2, D // 4 + 1, CW), i32),
            pltpu.VMEM((CH, 2, D // 4 + 1, CW), i32),
            pltpu.VMEM((XR, BW), f32),
            pltpu.VMEM((CH, 7, XR // 2 + 1, CW), i32),
            pltpu.VMEM((CH, 7, XR // 2 + 1, CW), i32),
            pltpu.VMEM((7, XR, BW), f32),
            pltpu.VMEM((XR, BW), f32),
            pltpu.VMEM((8, 128), f32),
            pltpu.VMEM((7, 8, 128), f32),
            pltpu.VMEM((8, 128), f32),
            pltpu.VMEM((7, 8, 128), f32),
            pltpu.VMEM((7, 7, BW), i32),
            pltpu.VMEM((7, 7, BW), i32),
            dma((6,)), dma, dma, dma, dma((3,)), dma, dma((2, CH)), dma, dma((CH, 2)), dma, dma((CH,)),
            dma, dma, dma, dma, dma, dma((7,)), pltpu.SemaphoreType.REGULAR((3,)),
        ],
        compiler_params=pltpu.CompilerParams(collective_id=0, has_side_effects=True, vmem_limit_bytes=53 * 2**20 + 700000),
        name="clipped_sum",
    )(activations[0, 0], out_grads[0, 0], kept_mask)
    clipped = own + rest[:ZR]
    update = (clipped + CLIP * noise_field) * (1.0 / IMAGES)
    return clipped, update, rest[ZR, :1]


def solution(mesh):
    in_specs = (
        P("img", "aug", None, None),
        P("img", "aug", None, None),
        P("img", "aug"),
        P("img", "aug"),
    )
    out_specs = (P("img", "aug"), P("img", "aug"), P("img"))
    return jax.shard_map(
        per_device, mesh=mesh, in_specs=in_specs, out_specs=out_specs, check_vma=False
    )
```

```python
import functools
import math

import jax
import jax.numpy as jnp
from jax import lax
from jax.experimental import pallas as pl
from jax.experimental.pallas import tpu as pltpu
from jax.sharding import PartitionSpec as P

MESH = pl.DeviceIdType.MESH
NZ, NX, NY = 16, 4, 4
S, D, FF = 197, 768, 3072
SP = 208
MAIN = 192
BW = FF // 8
CH = 3
CW = BW // CH
XR = D // 8
ZR = D // (NX * NZ)
IMAGES = 64
CLIP = 0.01 * math.sqrt(D * FF * S)
LEVELS = 32766.0
GROUP = ((2, 1), (2, 0), (1, 1), (1, 0), (3, 1), (3, 0), (0, 1), (0, 0))
Z_ORDER = (7, 6, 5, 4, 3, 2, 1, 0)


def kernel(
    a_hbm, g_hbm, m_hbm,
    own_ref, rest_ref,
    a_raw, g_raw, m_ref, tail32, tail_out, tail_in, a_all, a_perm, g_all, perm, half_sum, p_out, p_in, own_part, x_out, x_in, x_part, parts,
    stat_out, stat_in, fac_out, fac_in, z_out, z_in,
    in_sem, t_send, t_recv, a_send, a_recv, g_send, g_recv, p_send, p_recv, x_send, x_recv, s_send, s_recv, f_send, f_recv, z_send, z_recv, met,
):
    img, aug = lax.axis_index("img"), lax.axis_index("aug")
    z, x, y, c = img // NX, lax.rem(img, NX), aug // 2, lax.rem(aug, 2)

    mate = (1 - 2 * lax.rem(y, 2)) * (1 - 2 * c)

    def at_y(dy, dc):
        return (img, lax.rem(y + dy + NY, NY) * 2 + (lax.rem(c + dc, 2)))

    def block_of(dy, dc):
        return lax.rem(y + dy + NY, NY) * 2 + lax.rem(c + dc, 2)

    pair = z + 1 - 2 * lax.rem(z, 2)

    def z_step(of):
        return 1 - 2 * lax.rem(of + 1, 2)

    def in_group(dx, other):
        return ((pair if other else z) * NX + lax.rem(x + dx, NX), aug)

    def at_z(dz):
        return (lax.rem(z + dz + NZ, NZ) * NX + x, aug)

    partners = (
        (2, (mate, 0), ((2, 0), (mate, 0))),
        (3, (-mate, 1), ((2, 1), (-mate, 1))),
        (1, (0, 1), ((mate, 1), (0, 1))),
    )
    aug_peers = [(dy, dc) for dy in range(NY) for dc in range(2) if (dy, dc) != (0, 0)]

    barrier = pltpu.get_barrier_semaphore()
    next_to = [at_y(0, 1), at_y(1, 0), at_y(1, 1), at_y(-1, 0), at_y(-1, 1)]
    next_to += [in_group(1, 0), in_group(NX - 1, 0), at_z(1), at_z(-1)]
    for device in next_to:
        pl.semaphore_signal(barrier, inc=1, device_id=device, device_id_type=MESH)

    a_load = pltpu.make_async_copy(a_hbm, a_raw, in_sem.at[0])
    g_load = pltpu.make_async_copy(g_hbm, g_raw, in_sem.at[1])
    m_load = pltpu.make_async_copy(m_hbm, m_ref, in_sem.at[2])
    m_load.start()
    a_load.start()
    g_load.start()

    def columns(block, k, width):
        return pl.ds(pl.multiple_of(block * BW + k * CW, CW), width)

    own_copies = [pltpu.make_async_copy(a_hbm.at[pl.ds(0, MAIN)], a_all.at[0, pl.ds(0, MAIN)], in_sem.at[3])]
    for b, block in enumerate((block_of(-mate, 0), block_of(0, 0))):
        own_copies.append(pltpu.make_async_copy(
            g_hbm.at[pl.ds(0, MAIN), columns(block, 0, BW)], g_all.at[b, 0, pl.ds(0, MAIN)], in_sem.at[4 + b]))
    for copy in own_copies:
        copy.start()

    pl.semaphore_wait(barrier, 9)

    def call(step, devices):
        for device in devices:
            pl.semaphore_signal(met.at[step], inc=1, device_id=device, device_id_type=MESH)

    call(0, [at_y(1, 0), in_group(1, 0), in_group(NX - 1, 0), at_z(1), at_z(-1)])

    def whole(ref, sem):
        pltpu.make_async_copy(ref, ref, sem).wait()

    a_copies = []
    for slot, device, _ in partners:
        copy = pltpu.make_async_remote_copy(
            src_ref=a_hbm.at[pl.ds(0, MAIN)], dst_ref=a_all.at[slot, pl.ds(0, MAIN)],
            send_sem=a_send, recv_sem=a_recv.at[slot - 1], device_id=at_y(*device), device_id_type=MESH)
        copy.start()
        a_copies.append(copy)

    m_load.wait()
    mask = m_ref[...].astype(jnp.float32)
    a_load.wait()
    g_load.wait()
    tail32[...] = jnp.zeros_like(tail32)
    targets = [(0, (), ((-mate, 0), (0, 0)))] + list(partners)
    for i, (slot, device, blocks) in enumerate(targets):
        tail32[i, 0:S - MAIN, :] = a_raw[MAIN:S, :].astype(jnp.float32)
        tail32[i, 5:6, :] = jnp.broadcast_to(mask, (1, D))
        for b in range(2):
            tail32[i, 8:8 + S - MAIN, b * BW:(b + 1) * BW] = g_raw[
                MAIN:S, columns(block_of(*blocks[b]), 0, BW)].astype(jnp.float32)
        if slot == 0:
            tail_in[0] = tail32[i].astype(jnp.bfloat16)
            continue
        tail_out[i - 1] = tail32[i].astype(jnp.bfloat16)
        pltpu.make_async_remote_copy(
            src_ref=tail_out.at[i - 1], dst_ref=tail_in.at[slot], send_sem=t_send, recv_sem=t_recv,
            device_id=at_y(*device), device_id_type=MESH).start()

    for b in range(2):
        for k in range(CH):
            for slot, device, blocks in partners:
                copy = pltpu.make_async_remote_copy(
                    src_ref=g_raw.at[pl.ds(0, MAIN), columns(block_of(*blocks[b]), k, CW)],
                    dst_ref=g_all.at[b, slot, pl.ds(0, MAIN), pl.ds(k * CW, CW)],
                    send_sem=g_send, recv_sem=g_recv.at[b, k],
                    device_id=at_y(*device), device_id_type=MESH)
                copy.start()

    pl.semaphore_wait(met.at[0], 5)
    call(1, [in_group(1, 0), at_z(2), at_z(-2)])
    pl.semaphore_wait(met.at[1], 3)
    call(2, [at_z(4), at_z(-4)])

    p = lax.broadcasted_iota(jnp.int32, (1, D), 1)
    pn, pj, pr = p // XR, lax.rem(p, XR) // ZR, lax.rem(p, ZR)
    step_x = jnp.where(pn < 2, 2, jnp.where(pn < 4, 1, jnp.where(pn < 6, 3, 0)))
    from_z = jnp.where(lax.rem(pn, 2) == 0, pair, z)
    source = lax.rem(from_z + z_step(from_z) * pj + NZ, NZ) * (NX * ZR) + lax.rem(x + step_x, NX) * ZR + pr
    perm[...] = (lax.broadcasted_iota(jnp.int32, (D, D), 0) == source).astype(jnp.bfloat16)

    def permute(s):
        tail = tail_in[s].astype(jnp.float32)
        row = lax.broadcasted_iota(jnp.int32, (16, D), 0)
        a_all[s, MAIN:SP, :] = jnp.where(row < S - MAIN, tail, 0.0).astype(jnp.bfloat16)
        grads = jnp.where(row[0:8] < S - MAIN, tail[8:16], 0.0)
        grads = jnp.concatenate([grads, jnp.zeros((8, D), jnp.float32)], axis=0).astype(jnp.bfloat16)
        for b in range(2):
            g_all[b, s, MAIN:SP, :] = grads[:, b * BW:(b + 1) * BW]
        product = jnp.dot(a_all[s], perm[...], preferred_element_type=jnp.float32)
        a_perm[s * SP:(s + 1) * SP, :] = (product * tail[5:6, :]).astype(jnp.bfloat16)

    for copy in own_copies:
        copy.wait()
    permute(0)
    whole(tail_in.at[pl.ds(1, 3)], t_recv)
    for copy, slot in zip(reversed(a_copies), (1, 3, 2)):
        copy.wait_recv()
        permute(slot)

    def scale_of(level):
        return jnp.exp2(level.astype(jnp.float32) * (1.0 / 64.0))

    def pack(piece):
        half = piece.shape[0] // 2
        top = jnp.maximum(jnp.max(jnp.abs(piece), axis=0, keepdims=True), 1e-30)
        level = jnp.ceil(jnp.log2(top) * 64.0).astype(jnp.int32) + 1
        ints = jnp.round(piece * (LEVELS / scale_of(level))).astype(jnp.int32)
        return ints[:half] * 65536 + ints[half:], level

    def unpack(words, level, weight):
        high = (words + 32768) >> 16
        low = words - high * 65536
        scale = scale_of(level) * (weight * (1.0 / LEVELS))
        return high.astype(jnp.float32) * scale, low.astype(jnp.float32) * scale

    half = D // 2
    p_copies = {}
    for b in range(2):
        for k in range(CH):
            whole(g_all.at[b, pl.ds(1, 3), pl.ds(0, MAIN), pl.ds(k * CW, CW)], g_recv.at[b, k])
            cols = slice(k * CW, (k + 1) * CW)
            for h in range(2):
                block = lax.dot_general(
                    a_perm[:, h * half:(h + 1) * half], g_all[b, :, :, cols].reshape(4 * SP, CW), (((0,), (0,)), ((), ())),
                    preferred_element_type=jnp.float32)
                if b:
                    half_sum[h * half:(h + 1) * half, cols] = block
                    continue
                words, level = pack(block)
                p_out[k, h, 0:half // 2, :] = words
                p_out[k, h, half // 2:, :] = level
                copy = pltpu.make_async_remote_copy(
                    src_ref=p_out.at[k, h], dst_ref=p_in.at[k, h],
                    send_sem=p_send, recv_sem=p_recv.at[k, h], device_id=at_y(-mate, 0), device_id_type=MESH)
                copy.start()
                p_copies[k, h] = copy
    whole(a_all.at[pl.ds(1, 3), pl.ds(0, MAIN)], a_send)
    whole(g_all.at[:, pl.ds(1, 3), pl.ds(0, MAIN)], g_send)
    whole(tail_out, t_send)

    total = jnp.zeros((1, CW), jnp.float32)
    for k in range(CH):
        cols = slice(k * CW, (k + 1) * CW)
        for h in range(2):
            p_copies[k, h].wait_recv()
            parts_of = unpack(p_in[k, h, 0:half // 2, :], p_in[k, h, half // 2:half // 2 + 1, :], 1.0)
            block = jnp.concatenate(parts_of, axis=0) + half_sum[h * half:(h + 1) * half, cols]
            total = total + jnp.sum(block * block, axis=0, keepdims=True)
            if (k, h) == (CH - 1, 1):
                square = jnp.sum(total, axis=1, keepdims=True)
                row = lax.broadcasted_iota(jnp.int32, (8, 128), 0)
                stat = jnp.where(row < 4, jnp.broadcast_to(square, (8, 128)), jnp.broadcast_to(mask, (8, 128)))
                stat_out[...] = stat
                for i, (dy, dc) in enumerate(aug_peers):
                    copy = pltpu.make_async_remote_copy(
                        src_ref=stat_out, dst_ref=stat_in.at[i], send_sem=s_send, recv_sem=s_recv,
                        device_id=at_y(dy, dc), device_id_type=MESH)
                    copy.start()
            if h == 1:
                own_part[:, cols] = block[3 * XR:]
            for t in range(4 - h):
                words, level = pack(block[t * XR:(t + 1) * XR])
                n = h * 4 + t
                x_out[k, n, 0:XR // 2, :] = words
                x_out[k, n, XR // 2:, :] = level
                copy = pltpu.make_async_remote_copy(
                    src_ref=x_out.at[k, n], dst_ref=x_in.at[k, n],
                    send_sem=x_send, recv_sem=x_recv.at[k], device_id=in_group(*GROUP[n]), device_id_type=MESH)
                copy.start()

    pl.semaphore_wait(met.at[2], 2)

    whole(stat_in, s_recv)
    near = (stat + stat_in[0]) + (stat_in[3] + stat_in[4])
    far = (stat_in[1] + stat_in[2]) + (stat_in[5] + stat_in[6])
    stat = near + far
    count = stat[4:5, :]
    root = jnp.sqrt(stat[0:1, :])
    weight = CLIP / jnp.maximum(root, CLIP * count)
    fac_out[...] = jnp.broadcast_to(weight, (8, 128))
    for n in range(7):
        copy = pltpu.make_async_remote_copy(
            src_ref=fac_out, dst_ref=fac_in.at[n], send_sem=f_send, recv_sem=f_recv,
            device_id=in_group(*GROUP[n]), device_id_type=MESH)
        copy.start()

    rest_ref[ZR:ZR + 1, 0:128] = root / count
    half = XR // 2
    for k in range(CH):
        cols = slice(k * CW, (k + 1) * CW)
        whole(x_in.at[k], x_recv.at[k])
        for n in range(7):
            high, low = unpack(x_in[k, n, 0:half, :], x_in[k, n, half:half + 1, :], 1.0)
            x_part[n, 0:half, cols] = high
            x_part[n, half:, cols] = low
    whole(fac_in, f_recv)
    for k in range(CH):
        cols = slice(k * CW, (k + 1) * CW)
        part = weight * own_part[:, cols]
        for n in range(7):
            part = part + fac_in[n, 0:1, :] * x_part[n, :, cols]
        parts[:, cols] = part

    z_copies = []
    for d in Z_ORDER:
        words, level = pack(parts[d * ZR:(d + 1) * ZR, :])
        if d == 0:
            own_ref[0:6, :], own_ref[6:12, :] = unpack(words, level, 1.0)
            continue
        z_out[d - 1, 0:6, :] = words
        z_out[d - 1, 6:7, :] = level
        copy = pltpu.make_async_remote_copy(
            src_ref=z_out.at[d - 1], dst_ref=z_in.at[d - 1], send_sem=z_send, recv_sem=z_recv.at[d - 1],
            device_id=at_z(z_step(z) * d), device_id_type=MESH)
        copy.start()
        z_copies.append((d, copy))

    whole(p_out, p_send)
    whole(x_out, x_send)
    whole(stat_in, s_send)
    whole(fac_in, f_send)
    top_rows = low_rows = None
    for d, copy in reversed(z_copies):
        copy.wait_recv()
        words = z_in[d - 1]
        one, two = unpack(words[0:6], words[6:7], 1.0)
        top_rows = one if top_rows is None else top_rows + one
        low_rows = two if low_rows is None else low_rows + two
    rest_ref[0:6, :] = top_rows
    rest_ref[6:12, :] = low_rows

    whole(z_out, z_send)


def finish(own_ref, rest_ref, noise_ref, clip_ref, upd_ref, norm_ref):
    clipped = own_ref[...] + rest_ref[0:ZR, :]
    clip_ref[...] = clipped
    upd_ref[...] = (clipped + CLIP * noise_ref[...]) * (1.0 / IMAGES)
    norm_ref[0] = jnp.max(rest_ref[ZR:ZR + 1, 0:128])


def per_device(activations, out_grads, kept_mask, noise_field):
    vmem = pl.BlockSpec(memory_space=pltpu.VMEM)
    hbm = pl.BlockSpec(memory_space=pl.ANY)
    dma = pltpu.SemaphoreType.DMA
    bf16, f32, i32 = jnp.bfloat16, jnp.float32, jnp.int32
    own, rest = pl.pallas_call(
        kernel,
        out_shape=(jax.ShapeDtypeStruct((ZR, BW), f32), jax.ShapeDtypeStruct((16, BW), f32)),
        in_specs=[hbm, hbm, hbm],
        out_specs=(vmem,) * 2,
        scratch_shapes=[
            pltpu.VMEM((S, D), bf16),
            pltpu.VMEM((S, FF), bf16),
            pltpu.VMEM((1, 1), i32),
            pltpu.VMEM((4, 16, D), f32),
            pltpu.VMEM((3, 16, D), bf16),
            pltpu.VMEM((4, 16, D), bf16),
            pltpu.VMEM((4, SP, D), bf16),
            pltpu.VMEM((4 * SP, D), bf16),
            pltpu.VMEM((2, 4, SP, BW), bf16),
            pltpu.VMEM((D, D), bf16),
            pltpu.VMEM((D, BW), f32),
            pltpu.VMEM((CH, 2, D // 4 + 1, CW), i32),
            pltpu.VMEM((CH, 2, D // 4 + 1, CW), i32),
            pltpu.VMEM((XR, BW), f32),
            pltpu.VMEM((CH, 7, XR // 2 + 1, CW), i32),
            pltpu.VMEM((CH, 7, XR // 2 + 1, CW), i32),
            pltpu.VMEM((7, XR, BW), f32),
            pltpu.VMEM((XR, BW), f32),
            pltpu.VMEM((8, 128), f32),
            pltpu.VMEM((7, 8, 128), f32),
            pltpu.VMEM((8, 128), f32),
            pltpu.VMEM((7, 8, 128), f32),
            pltpu.VMEM((7, 7, BW), i32),
            pltpu.VMEM((7, 7, BW), i32),
            dma((6,)), dma, dma, dma, dma((3,)), dma, dma((2, CH)), dma, dma((CH, 2)), dma, dma((CH,)),
            dma, dma, dma, dma, dma, dma((7,)), pltpu.SemaphoreType.REGULAR((3,)),
        ],
        compiler_params=pltpu.CompilerParams(collective_id=0, has_side_effects=True, vmem_limit_bytes=53 * 2**20 + 700000),
        name="clipped_sum",
    )(activations[0, 0], out_grads[0, 0], kept_mask)
    clipped, update, norm = pl.pallas_call(
        finish,
        out_shape=(
            jax.ShapeDtypeStruct((ZR, BW), f32), jax.ShapeDtypeStruct((ZR, BW), f32), jax.ShapeDtypeStruct((1,), f32)),
        in_specs=[vmem] * 3,
        out_specs=(vmem, vmem, pl.BlockSpec(memory_space=pltpu.SMEM)),
        compiler_params=pltpu.CompilerParams(vmem_limit_bytes=2**20),
        name="update",
    )(own, rest, noise_field)
    return clipped, update, norm


def solution(mesh):
    in_specs = (
        P("img", "aug", None, None),
        P("img", "aug", None, None),
        P("img", "aug"),
        P("img", "aug"),
    )
    out_specs = (P("img", "aug"), P("img", "aug"), P("img"))
    return jax.shard_map(
        per_device, mesh=mesh, in_specs=in_specs, out_specs=out_specs, check_vma=False
    )
```

```python
import functools
import math

import jax
import jax.numpy as jnp
from jax import lax
from jax.experimental import pallas as pl
from jax.experimental.pallas import tpu as pltpu
from jax.sharding import PartitionSpec as P

MESH = pl.DeviceIdType.MESH
NZ, NX, NY = 16, 4, 4
S, D, FF = 197, 768, 3072
SP = 208
MAIN = 192
BW = FF // 8
CH = 3
CW = BW // CH
XR = D // 8
ZR = D // (NX * NZ)
IMAGES = 64
CLIP = 0.01 * math.sqrt(D * FF * S)
LEVELS = 32766.0
GROUP = ((2, 1), (2, 0), (1, 1), (1, 0), (3, 1), (3, 0), (0, 1), (0, 0))
Z_ORDER = (7, 6, 5, 4, 3, 2, 1, 0)


def kernel(
    a_hbm, g_hbm, m_hbm,
    own_ref, rest_ref,
    a_raw, g_raw, m_ref, tail32, tail_out, tail_in, a_all, a_perm, g_all, perm, half_sum, p_out, p_in, own_part, x_out, x_in, x_part, parts,
    stat_out, stat_in, fac_out, fac_in, z_out, z_in,
    in_sem, t_send, t_recv, a_send, a_recv, g_send, g_recv, p_send, p_recv, x_send, x_recv, s_send, s_recv, f_send, f_recv, z_send, z_recv, met,
):
    img, aug = lax.axis_index("img"), lax.axis_index("aug")
    z, x, y, c = img // NX, lax.rem(img, NX), aug // 2, lax.rem(aug, 2)

    mate = (1 - 2 * lax.rem(y, 2)) * (1 - 2 * c)

    def at_y(dy, dc):
        return (img, lax.rem(y + dy + NY, NY) * 2 + (lax.rem(c + dc, 2)))

    def block_of(dy, dc):
        return lax.rem(y + dy + NY, NY) * 2 + lax.rem(c + dc, 2)

    pair = z + 1 - 2 * lax.rem(z, 2)

    def z_step(of):
        return 1 - 2 * lax.rem(of + 1, 2)

    def in_group(dx, other):
        return ((pair if other else z) * NX + lax.rem(x + dx, NX), aug)

    def at_z(dz):
        return (lax.rem(z + dz + NZ, NZ) * NX + x, aug)

    partners = (
        (2, (mate, 0), ((2, 0), (mate, 0))),
        (3, (-mate, 1), ((2, 1), (-mate, 1))),
        (1, (0, 1), ((mate, 1), (0, 1))),
    )
    aug_peers = [(dy, dc) for dy in range(NY) for dc in range(2) if (dy, dc) != (0, 0)]

    barrier = pltpu.get_barrier_semaphore()
    next_to = [at_y(0, 1), at_y(1, 0), at_y(1, 1), at_y(-1, 0), at_y(-1, 1)]
    next_to += [in_group(1, 0), in_group(NX - 1, 0), at_z(1), at_z(-1)]
    for device in next_to:
        pl.semaphore_signal(barrier, inc=1, device_id=device, device_id_type=MESH)

    pl.semaphore_wait(barrier, 9)

    def call(step, devices):
        for device in devices:
            pl.semaphore_signal(met.at[step], inc=1, device_id=device, device_id_type=MESH)

    def whole(ref, sem):
        pltpu.make_async_copy(ref, ref, sem).wait()

    a_copies = []
    for slot, device, _ in partners:
        copy = pltpu.make_async_remote_copy(
            src_ref=a_hbm.at[pl.ds(0, MAIN)], dst_ref=a_all.at[slot, pl.ds(0, MAIN)],
            send_sem=a_send, recv_sem=a_recv.at[slot - 1], device_id=at_y(*device), device_id_type=MESH)
        copy.start()
        a_copies.append(copy)

    call(0, [at_y(1, 0), in_group(1, 0), in_group(NX - 1, 0), at_z(1), at_z(-1)])

    a_load = pltpu.make_async_copy(a_hbm, a_raw, in_sem.at[0])
    g_load = pltpu.make_async_copy(g_hbm, g_raw, in_sem.at[1])
    m_load = pltpu.make_async_copy(m_hbm, m_ref, in_sem.at[2])
    m_load.start()
    a_load.start()
    g_load.start()

    def columns(block, k, width):
        return pl.ds(pl.multiple_of(block * BW + k * CW, CW), width)

    own_copies = [pltpu.make_async_copy(a_hbm.at[pl.ds(0, MAIN)], a_all.at[0, pl.ds(0, MAIN)], in_sem.at[3])]
    for b, block in enumerate((block_of(-mate, 0), block_of(0, 0))):
        own_copies.append(pltpu.make_async_copy(
            g_hbm.at[pl.ds(0, MAIN), columns(block, 0, BW)], g_all.at[b, 0, pl.ds(0, MAIN)], in_sem.at[4 + b]))
    for copy in own_copies:
        copy.start()

    m_load.wait()
    mask = m_ref[...].astype(jnp.float32)
    a_load.wait()
    g_load.wait()
    tail32[...] = jnp.zeros_like(tail32)
    targets = [(0, (), ((-mate, 0), (0, 0)))] + list(partners)
    for i, (slot, device, blocks) in enumerate(targets):
        tail32[i, 0:S - MAIN, :] = a_raw[MAIN:S, :].astype(jnp.float32)
        tail32[i, 5:6, :] = jnp.broadcast_to(mask, (1, D))
        for b in range(2):
            tail32[i, 8:8 + S - MAIN, b * BW:(b + 1) * BW] = g_raw[
                MAIN:S, columns(block_of(*blocks[b]), 0, BW)].astype(jnp.float32)
        if slot == 0:
            tail_in[0] = tail32[i].astype(jnp.bfloat16)
            continue
        tail_out[i - 1] = tail32[i].astype(jnp.bfloat16)
        pltpu.make_async_remote_copy(
            src_ref=tail_out.at[i - 1], dst_ref=tail_in.at[slot], send_sem=t_send, recv_sem=t_recv,
            device_id=at_y(*device), device_id_type=MESH).start()

    for b in range(2):
        for k in range(CH):
            for slot, device, blocks in partners:
                copy = pltpu.make_async_remote_copy(
                    src_ref=g_raw.at[pl.ds(0, MAIN), columns(block_of(*blocks[b]), k, CW)],
                    dst_ref=g_all.at[b, slot, pl.ds(0, MAIN), pl.ds(k * CW, CW)],
                    send_sem=g_send, recv_sem=g_recv.at[b, k],
                    device_id=at_y(*device), device_id_type=MESH)
                copy.start()

    pl.semaphore_wait(met.at[0], 5)
    call(1, [in_group(1, 0), at_z(2), at_z(-2)])
    pl.semaphore_wait(met.at[1], 3)
    call(2, [at_z(4), at_z(-4)])

    p = lax.broadcasted_iota(jnp.int32, (1, D), 1)
    pn, pj, pr = p // XR, lax.rem(p, XR) // ZR, lax.rem(p, ZR)
    step_x = jnp.where(pn < 2, 2, jnp.where(pn < 4, 1, jnp.where(pn < 6, 3, 0)))
    from_z = jnp.where(lax.rem(pn, 2) == 0, pair, z)
    source = lax.rem(from_z + z_step(from_z) * pj + NZ, NZ) * (NX * ZR) + lax.rem(x + step_x, NX) * ZR + pr
    perm[...] = (lax.broadcasted_iota(jnp.int32, (D, D), 0) == source).astype(jnp.bfloat16)

    def permute(s):
        tail = tail_in[s].astype(jnp.float32)
        row = lax.broadcasted_iota(jnp.int32, (16, D), 0)
        a_all[s, MAIN:SP, :] = jnp.where(row < S - MAIN, tail, 0.0).astype(jnp.bfloat16)
        grads = jnp.where(row[0:8] < S - MAIN, tail[8:16], 0.0)
        grads = jnp.concatenate([grads, jnp.zeros((8, D), jnp.float32)], axis=0).astype(jnp.bfloat16)
        for b in range(2):
            g_all[b, s, MAIN:SP, :] = grads[:, b * BW:(b + 1) * BW]
        product = jnp.dot(a_all[s], perm[...], preferred_element_type=jnp.float32)
        a_perm[s * SP:(s + 1) * SP, :] = (product * tail[5:6, :]).astype(jnp.bfloat16)

    for copy in own_copies:
        copy.wait()
    permute(0)
    whole(tail_in.at[pl.ds(1, 3)], t_recv)
    for copy, slot in zip(reversed(a_copies), (1, 3, 2)):
        copy.wait_recv()
        permute(slot)

    def scale_of(level):
        return jnp.exp2(level.astype(jnp.float32) * (1.0 / 64.0))

    def pack(piece):
        half = piece.shape[0] // 2
        top = jnp.maximum(jnp.max(jnp.abs(piece), axis=0, keepdims=True), 1e-30)
        level = jnp.ceil(jnp.log2(top) * 64.0).astype(jnp.int32) + 1
        ints = jnp.round(piece * (LEVELS / scale_of(level))).astype(jnp.int32)
        return ints[:half] * 65536 + ints[half:], level

    def unpack(words, level, weight):
        high = (words + 32768) >> 16
        low = words - high * 65536
        scale = scale_of(level) * (weight * (1.0 / LEVELS))
        return high.astype(jnp.float32) * scale, low.astype(jnp.float32) * scale

    half = D // 2
    p_copies = {}
    for b in range(2):
        for k in range(CH):
            whole(g_all.at[b, pl.ds(1, 3), pl.ds(0, MAIN), pl.ds(k * CW, CW)], g_recv.at[b, k])
            cols = slice(k * CW, (k + 1) * CW)
            for h in range(2):
                block = lax.dot_general(
                    a_perm[:, h * half:(h + 1) * half], g_all[b, :, :, cols].reshape(4 * SP, CW), (((0,), (0,)), ((), ())),
                    preferred_element_type=jnp.float32)
                if b:
                    half_sum[h * half:(h + 1) * half, cols] = block
                    continue
                words, level = pack(block)
                p_out[k, h, 0:half // 2, :] = words
                p_out[k, h, half // 2:, :] = level
                copy = pltpu.make_async_remote_copy(
                    src_ref=p_out.at[k, h], dst_ref=p_in.at[k, h],
                    send_sem=p_send, recv_sem=p_recv.at[k, h], device_id=at_y(-mate, 0), device_id_type=MESH)
                copy.start()
                p_copies[k, h] = copy
    whole(a_all.at[pl.ds(1, 3), pl.ds(0, MAIN)], a_send)
    whole(g_all.at[:, pl.ds(1, 3), pl.ds(0, MAIN)], g_send)
    whole(tail_out, t_send)

    total = jnp.zeros((1, CW), jnp.float32)
    for k in range(CH):
        cols = slice(k * CW, (k + 1) * CW)
        for h in range(2):
            p_copies[k, h].wait_recv()
            parts_of = unpack(p_in[k, h, 0:half // 2, :], p_in[k, h, half // 2:half // 2 + 1, :], 1.0)
            high = parts_of[0] + half_sum[h * half:h * half + half // 2, cols]
            low = parts_of[1] + half_sum[h * half + half // 2:(h + 1) * half, cols]
            total = total + jnp.sum(high * high + low * low, axis=0, keepdims=True)
            block = jnp.concatenate([high, low], axis=0)
            if (k, h) == (CH - 1, 1):
                square = jnp.sum(total, axis=1, keepdims=True)
                row = lax.broadcasted_iota(jnp.int32, (8, 128), 0)
                stat = jnp.where(row < 4, jnp.broadcast_to(square, (8, 128)), jnp.broadcast_to(mask, (8, 128)))
                stat_out[...] = stat
                for i in (3, 4, 1, 2, 5, 6, 0):
                    dy, dc = aug_peers[i]
                    copy = pltpu.make_async_remote_copy(
                        src_ref=stat_out, dst_ref=stat_in.at[i], send_sem=s_send, recv_sem=s_recv,
                        device_id=at_y(dy, dc), device_id_type=MESH)
                    copy.start()
            if h == 1:
                own_part[:, cols] = block[3 * XR:]
            for t in range(4 - h):
                words, level = pack(block[t * XR:(t + 1) * XR])
                n = h * 4 + t
                x_out[k, n, 0:XR // 2, :] = words
                x_out[k, n, XR // 2:, :] = level
                copy = pltpu.make_async_remote_copy(
                    src_ref=x_out.at[k, n], dst_ref=x_in.at[k, n],
                    send_sem=x_send, recv_sem=x_recv.at[k], device_id=in_group(*GROUP[n]), device_id_type=MESH)
                copy.start()

    pl.semaphore_wait(met.at[2], 2)

    whole(stat_in, s_recv)
    near = (stat + stat_in[0]) + (stat_in[3] + stat_in[4])
    far = (stat_in[1] + stat_in[2]) + (stat_in[5] + stat_in[6])
    stat = near + far
    count = stat[4:5, :]
    root = jnp.sqrt(stat[0:1, :])
    weight = CLIP / jnp.maximum(root, CLIP * count)
    fac_out[...] = jnp.broadcast_to(weight, (8, 128))
    for n in range(7):
        copy = pltpu.make_async_remote_copy(
            src_ref=fac_out, dst_ref=fac_in.at[n], send_sem=f_send, recv_sem=f_recv,
            device_id=in_group(*GROUP[n]), device_id_type=MESH)
        copy.start()

    rest_ref[ZR:ZR + 1, 0:128] = root / count
    half = XR // 2
    for k in range(CH):
        cols = slice(k * CW, (k + 1) * CW)
        whole(x_in.at[k], x_recv.at[k])
        for n in range(7):
            high, low = unpack(x_in[k, n, 0:half, :], x_in[k, n, half:half + 1, :], 1.0)
            x_part[n, 0:half, cols] = high
            x_part[n, half:, cols] = low
    whole(fac_in, f_recv)
    for k in range(CH):
        cols = slice(k * CW, (k + 1) * CW)
        part = weight * own_part[:, cols]
        for n in range(7):
            part = part + fac_in[n, 0:1, :] * x_part[n, :, cols]
        parts[:, cols] = part

    z_copies = []
    for d in Z_ORDER:
        words, level = pack(parts[d * ZR:(d + 1) * ZR, :])
        if d == 0:
            own_ref[0:6, :], own_ref[6:12, :] = unpack(words, level, 1.0)
            continue
        z_out[d - 1, 0:6, :] = words
        z_out[d - 1, 6:7, :] = level
        copy = pltpu.make_async_remote_copy(
            src_ref=z_out.at[d - 1], dst_ref=z_in.at[d - 1], send_sem=z_send, recv_sem=z_recv.at[d - 1],
            device_id=at_z(z_step(z) * d), device_id_type=MESH)
        copy.start()
        z_copies.append((d, copy))

    whole(p_out, p_send)
    whole(x_out, x_send)
    whole(stat_in, s_send)
    whole(fac_in, f_send)
    top_rows = low_rows = None
    for d, copy in reversed(z_copies):
        copy.wait_recv()
        words = z_in[d - 1]
        one, two = unpack(words[0:6], words[6:7], 1.0)
        top_rows = one if top_rows is None else top_rows + one
        low_rows = two if low_rows is None else low_rows + two
    rest_ref[0:6, :] = top_rows
    rest_ref[6:12, :] = low_rows

    whole(z_out, z_send)


def finish(own_ref, rest_ref, noise_ref, clip_ref, upd_ref, norm_ref):
    clipped = own_ref[...] + rest_ref[0:ZR, :]
    clip_ref[...] = clipped
    upd_ref[...] = (clipped + CLIP * noise_ref[...]) * (1.0 / IMAGES)
    norm_ref[0] = jnp.max(rest_ref[ZR:ZR + 1, 0:128])


def per_device(activations, out_grads, kept_mask, noise_field):
    vmem = pl.BlockSpec(memory_space=pltpu.VMEM)
    hbm = pl.BlockSpec(memory_space=pl.ANY)
    dma = pltpu.SemaphoreType.DMA
    bf16, f32, i32 = jnp.bfloat16, jnp.float32, jnp.int32
    own, rest = pl.pallas_call(
        kernel,
        out_shape=(jax.ShapeDtypeStruct((ZR, BW), f32), jax.ShapeDtypeStruct((16, BW), f32)),
        in_specs=[hbm, hbm, hbm],
        out_specs=(vmem,) * 2,
        scratch_shapes=[
            pltpu.VMEM((S, D), bf16),
            pltpu.VMEM((S, FF), bf16),
            pltpu.VMEM((1, 1), i32),
            pltpu.VMEM((4, 16, D), f32),
            pltpu.VMEM((3, 16, D), bf16),
            pltpu.VMEM((4, 16, D), bf16),
            pltpu.VMEM((4, SP, D), bf16),
            pltpu.VMEM((4 * SP, D), bf16),
            pltpu.VMEM((2, 4, SP, BW), bf16),
            pltpu.VMEM((D, D), bf16),
            pltpu.VMEM((D, BW), f32),
            pltpu.VMEM((CH, 2, D // 4 + 1, CW), i32),
            pltpu.VMEM((CH, 2, D // 4 + 1, CW), i32),
            pltpu.VMEM((XR, BW), f32),
            pltpu.VMEM((CH, 7, XR // 2 + 1, CW), i32),
            pltpu.VMEM((CH, 7, XR // 2 + 1, CW), i32),
            pltpu.VMEM((7, XR, BW), f32),
            pltpu.VMEM((XR, BW), f32),
            pltpu.VMEM((8, 128), f32),
            pltpu.VMEM((7, 8, 128), f32),
            pltpu.VMEM((8, 128), f32),
            pltpu.VMEM((7, 8, 128), f32),
            pltpu.VMEM((7, 7, BW), i32),
            pltpu.VMEM((7, 7, BW), i32),
            dma((6,)), dma, dma, dma, dma((3,)), dma, dma((2, CH)), dma, dma((CH, 2)), dma, dma((CH,)),
            dma, dma, dma, dma, dma, dma((7,)), pltpu.SemaphoreType.REGULAR((3,)),
        ],
        compiler_params=pltpu.CompilerParams(collective_id=0, has_side_effects=True, vmem_limit_bytes=53 * 2**20 + 700000),
        name="clipped_sum",
    )(activations[0, 0], out_grads[0, 0], kept_mask)
    clipped, update, norm = pl.pallas_call(
        finish,
        out_shape=(
            jax.ShapeDtypeStruct((ZR, BW), f32), jax.ShapeDtypeStruct((ZR, BW), f32), jax.ShapeDtypeStruct((1,), f32)),
        in_specs=[vmem] * 3,
        out_specs=(vmem, vmem, pl.BlockSpec(memory_space=pltpu.SMEM)),
        compiler_params=pltpu.CompilerParams(vmem_limit_bytes=2**20),
        name="update",
    )(own, rest, noise_field)
    return clipped, update, norm


def solution(mesh):
    in_specs = (
        P("img", "aug", None, None),
        P("img", "aug", None, None),
        P("img", "aug"),
        P("img", "aug"),
    )
    out_specs = (P("img", "aug"), P("img", "aug"), P("img"))
    return jax.shard_map(
        per_device, mesh=mesh, in_specs=in_specs, out_specs=out_specs, check_vma=False
    )
```

```python
import functools
import math

import jax
import jax.numpy as jnp
from jax import lax
from jax.experimental import pallas as pl
from jax.experimental.pallas import tpu as pltpu
from jax.sharding import PartitionSpec as P

MESH = pl.DeviceIdType.MESH
NZ, NX, NY = 16, 4, 4
S, D, FF = 197, 768, 3072
SP = 208
MAIN = 192
BW = FF // 8
CH = 3
CW = BW // CH
XR = D // 8
ZR = D // (NX * NZ)
IMAGES = 64
CLIP = 0.01 * math.sqrt(D * FF * S)
LEVELS = 32766.0
GROUP = ((2, 1), (2, 0), (1, 1), (1, 0), (3, 1), (3, 0), (0, 1), (0, 0))
Z_ORDER = (7, 6, 5, 4, 3, 2, 1, 0)


def kernel(
    a_hbm, g_hbm, m_hbm,
    own_ref, rest_ref,
    a_raw, g_raw, m_ref, tail32, tail_out, tail_in, a_all, a_perm, g_all, perm, half_sum, p_out, p_in, own_part, x_out, x_in, x_part, parts,
    stat_out, stat_in, fac_out, fac_in, z_out, z_in,
    in_sem, t_send, t_recv, a_send, a_recv, g_send, g_recv, p_send, p_recv, x_send, x_recv, s_send, s_recv, f_send, f_recv, z_send, z_recv, met,
):
    img, aug = lax.axis_index("img"), lax.axis_index("aug")
    z, x, y, c = img // NX, lax.rem(img, NX), aug // 2, lax.rem(aug, 2)

    mate = (1 - 2 * lax.rem(y, 2)) * (1 - 2 * c)

    def at_y(dy, dc):
        return (img, lax.rem(y + dy + NY, NY) * 2 + (lax.rem(c + dc, 2)))

    def block_of(dy, dc):
        return lax.rem(y + dy + NY, NY) * 2 + lax.rem(c + dc, 2)

    pair = z + 1 - 2 * lax.rem(z, 2)

    def z_step(of):
        return 1 - 2 * lax.rem(of + 1, 2)

    def in_group(dx, other):
        return ((pair if other else z) * NX + lax.rem(x + dx, NX), aug)

    def at_z(dz):
        return (lax.rem(z + dz + NZ, NZ) * NX + x, aug)

    partners = (
        (2, (mate, 0), ((2, 0), (mate, 0))),
        (3, (-mate, 1), ((2, 1), (-mate, 1))),
        (1, (0, 1), ((mate, 1), (0, 1))),
    )
    aug_peers = [(dy, dc) for dy in range(NY) for dc in range(2) if (dy, dc) != (0, 0)]

    barrier = pltpu.get_barrier_semaphore()
    next_to = [at_y(0, 1), at_y(1, 0), at_y(1, 1), at_y(-1, 0), at_y(-1, 1)]
    next_to += [in_group(1, 0), in_group(NX - 1, 0), at_z(1), at_z(-1)]
    for device in next_to:
        pl.semaphore_signal(barrier, inc=1, device_id=device, device_id_type=MESH)

    pl.semaphore_wait(barrier, 9)

    def call(step, devices):
        for device in devices:
            pl.semaphore_signal(met.at[step], inc=1, device_id=device, device_id_type=MESH)

    def whole(ref, sem):
        pltpu.make_async_copy(ref, ref, sem).wait()

    a_copies = []
    for slot, device, _ in partners:
        copy = pltpu.make_async_remote_copy(
            src_ref=a_hbm.at[pl.ds(0, MAIN)], dst_ref=a_all.at[slot, pl.ds(0, MAIN)],
            send_sem=a_send, recv_sem=a_recv.at[slot - 1], device_id=at_y(*device), device_id_type=MESH)
        copy.start()
        a_copies.append(copy)

    call(0, [at_y(1, 0), in_group(1, 0), in_group(NX - 1, 0), at_z(1), at_z(-1)])

    a_load = pltpu.make_async_copy(a_hbm, a_raw, in_sem.at[0])
    g_load = pltpu.make_async_copy(g_hbm, g_raw, in_sem.at[1])
    m_load = pltpu.make_async_copy(m_hbm, m_ref, in_sem.at[2])
    m_load.start()
    a_load.start()
    g_load.start()

    def columns(block, k, width):
        return pl.ds(pl.multiple_of(block * BW + k * CW, CW), width)

    own_copies = [pltpu.make_async_copy(a_hbm.at[pl.ds(0, MAIN)], a_all.at[0, pl.ds(0, MAIN)], in_sem.at[3])]
    for b, block in enumerate((block_of(-mate, 0), block_of(0, 0))):
        own_copies.append(pltpu.make_async_copy(
            g_hbm.at[pl.ds(0, MAIN), columns(block, 0, BW)], g_all.at[b, 0, pl.ds(0, MAIN)], in_sem.at[4 + b]))
    for copy in own_copies:
        copy.start()

    m_load.wait()
    mask = m_ref[...].astype(jnp.float32)
    a_load.wait()
    g_load.wait()
    tail32[...] = jnp.zeros_like(tail32)
    targets = [(0, (), ((-mate, 0), (0, 0)))] + list(partners)
    for i, (slot, device, blocks) in enumerate(targets):
        tail32[i, 0:S - MAIN, :] = a_raw[MAIN:S, :].astype(jnp.float32)
        tail32[i, 5:6, :] = jnp.broadcast_to(mask, (1, D))
        for b in range(2):
            tail32[i, 8:8 + S - MAIN, b * BW:(b + 1) * BW] = g_raw[
                MAIN:S, columns(block_of(*blocks[b]), 0, BW)].astype(jnp.float32)
        if slot == 0:
            tail_in[0] = tail32[i].astype(jnp.bfloat16)
            continue
        tail_out[i - 1] = tail32[i].astype(jnp.bfloat16)
        pltpu.make_async_remote_copy(
            src_ref=tail_out.at[i - 1], dst_ref=tail_in.at[slot], send_sem=t_send, recv_sem=t_recv,
            device_id=at_y(*device), device_id_type=MESH).start()

    for b in range(2):
        for k in range(CH if b == 0 else 1):
            width = CW if b == 0 else BW
            for slot, device, blocks in partners:
                copy = pltpu.make_async_remote_copy(
                    src_ref=g_raw.at[pl.ds(0, MAIN), columns(block_of(*blocks[b]), k, width)],
                    dst_ref=g_all.at[b, slot, pl.ds(0, MAIN), pl.ds(k * CW, width)],
                    send_sem=g_send, recv_sem=g_recv.at[k if b == 0 else CH],
                    device_id=at_y(*device), device_id_type=MESH)
                copy.start()

    pl.semaphore_wait(met.at[0], 5)
    call(1, [in_group(1, 0), at_z(2), at_z(-2)])
    pl.semaphore_wait(met.at[1], 3)
    call(2, [at_z(4), at_z(-4)])

    p = lax.broadcasted_iota(jnp.int32, (1, D), 1)
    pn, pj, pr = p // XR, lax.rem(p, XR) // ZR, lax.rem(p, ZR)
    step_x = jnp.where(pn < 2, 2, jnp.where(pn < 4, 1, jnp.where(pn < 6, 3, 0)))
    from_z = jnp.where(lax.rem(pn, 2) == 0, pair, z)
    source = lax.rem(from_z + z_step(from_z) * pj + NZ, NZ) * (NX * ZR) + lax.rem(x + step_x, NX) * ZR + pr
    perm[...] = (lax.broadcasted_iota(jnp.int32, (D, D), 0) == source).astype(jnp.bfloat16)

    def permute(s):
        tail = tail_in[s].astype(jnp.float32)
        row = lax.broadcasted_iota(jnp.int32, (16, D), 0)
        a_all[s, MAIN:SP, :] = jnp.where(row < S - MAIN, tail, 0.0).astype(jnp.bfloat16)
        grads = jnp.where(row[0:8] < S - MAIN, tail[8:16], 0.0)
        grads = jnp.concatenate([grads, jnp.zeros((8, D), jnp.float32)], axis=0).astype(jnp.bfloat16)
        for b in range(2):
            g_all[b, s, MAIN:SP, :] = grads[:, b * BW:(b + 1) * BW]
        product = jnp.dot(a_all[s], perm[...], preferred_element_type=jnp.float32)
        a_perm[s * SP:(s + 1) * SP, :] = (product * tail[5:6, :]).astype(jnp.bfloat16)

    for copy in own_copies:
        copy.wait()
    permute(0)
    whole(tail_in.at[pl.ds(1, 3)], t_recv)
    for copy, slot in zip(reversed(a_copies), (1, 3, 2)):
        copy.wait_recv()
        permute(slot)

    def scale_of(level):
        return jnp.exp2(level.astype(jnp.float32) * (1.0 / 64.0))

    def pack(piece):
        half = piece.shape[0] // 2
        top = jnp.maximum(jnp.max(jnp.abs(piece), axis=0, keepdims=True), 1e-30)
        level = jnp.ceil(jnp.log2(top) * 64.0).astype(jnp.int32) + 1
        ints = jnp.round(piece * (LEVELS / scale_of(level))).astype(jnp.int32)
        return ints[:half] * 65536 + ints[half:], level

    def unpack(words, level, weight):
        high = (words + 32768) >> 16
        low = words - high * 65536
        scale = scale_of(level) * (weight * (1.0 / LEVELS))
        return high.astype(jnp.float32) * scale, low.astype(jnp.float32) * scale

    half = D // 2
    p_copies = {}
    for b in range(2):
        for k in range(CH):
            if b == 0:
                whole(g_all.at[0, pl.ds(1, 3), pl.ds(0, MAIN), pl.ds(k * CW, CW)], g_recv.at[k])
            elif k == 0:
                whole(g_all.at[1, pl.ds(1, 3), pl.ds(0, MAIN)], g_recv.at[CH])
            cols = slice(k * CW, (k + 1) * CW)
            for h in range(2):
                block = lax.dot_general(
                    a_perm[:, h * half:(h + 1) * half], g_all[b, :, :, cols].reshape(4 * SP, CW), (((0,), (0,)), ((), ())),
                    preferred_element_type=jnp.float32)
                if b:
                    half_sum[h * half:(h + 1) * half, cols] = block
                    continue
                words, level = pack(block)
                p_out[k, h, 0:half // 2, :] = words
                p_out[k, h, half // 2:, :] = level
                copy = pltpu.make_async_remote_copy(
                    src_ref=p_out.at[k, h], dst_ref=p_in.at[k, h],
                    send_sem=p_send, recv_sem=p_recv.at[k, h], device_id=at_y(-mate, 0), device_id_type=MESH)
                copy.start()
                p_copies[k, h] = copy
    whole(a_all.at[pl.ds(1, 3), pl.ds(0, MAIN)], a_send)
    whole(g_all.at[:, pl.ds(1, 3), pl.ds(0, MAIN)], g_send)
    whole(tail_out, t_send)

    total = jnp.zeros((1, CW), jnp.float32)
    for k in range(CH):
        cols = slice(k * CW, (k + 1) * CW)
        for h in range(2):
            p_copies[k, h].wait_recv()
            parts_of = unpack(p_in[k, h, 0:half // 2, :], p_in[k, h, half // 2:half // 2 + 1, :], 1.0)
            high = parts_of[0] + half_sum[h * half:h * half + half // 2, cols]
            low = parts_of[1] + half_sum[h * half + half // 2:(h + 1) * half, cols]
            total = total + jnp.sum(high * high + low * low, axis=0, keepdims=True)
            block = jnp.concatenate([high, low], axis=0)
            if (k, h) == (CH - 1, 1):
                square = jnp.sum(total, axis=1, keepdims=True)
                row = lax.broadcasted_iota(jnp.int32, (8, 128), 0)
                stat = jnp.where(row < 4, jnp.broadcast_to(square, (8, 128)), jnp.broadcast_to(mask, (8, 128)))
                stat_out[...] = stat
                for i in (3, 4, 1, 2, 5, 6, 0):
                    dy, dc = aug_peers[i]
                    copy = pltpu.make_async_remote_copy(
                        src_ref=stat_out, dst_ref=stat_in.at[i], send_sem=s_send, recv_sem=s_recv,
                        device_id=at_y(dy, dc), device_id_type=MESH)
                    copy.start()
            if h == 1:
                own_part[:, cols] = block[3 * XR:]
            for t in range(4 - h):
                words, level = pack(block[t * XR:(t + 1) * XR])
                n = h * 4 + t
                x_out[k, n, 0:XR // 2, :] = words
                x_out[k, n, XR // 2:, :] = level
                copy = pltpu.make_async_remote_copy(
                    src_ref=x_out.at[k, n], dst_ref=x_in.at[k, n],
                    send_sem=x_send, recv_sem=x_recv.at[k], device_id=in_group(*GROUP[n]), device_id_type=MESH)
                copy.start()

    pl.semaphore_wait(met.at[2], 2)

    whole(stat_in, s_recv)
    near = (stat + stat_in[0]) + (stat_in[3] + stat_in[4])
    far = (stat_in[1] + stat_in[2]) + (stat_in[5] + stat_in[6])
    stat = near + far
    count = stat[4:5, :]
    root = jnp.sqrt(stat[0:1, :])
    weight = CLIP / jnp.maximum(root, CLIP * count)
    fac_out[...] = jnp.broadcast_to(weight, (8, 128))
    for n in range(7):
        copy = pltpu.make_async_remote_copy(
            src_ref=fac_out, dst_ref=fac_in.at[n], send_sem=f_send, recv_sem=f_recv,
            device_id=in_group(*GROUP[n]), device_id_type=MESH)
        copy.start()

    rest_ref[ZR:ZR + 1, 0:128] = root / count
    half = XR // 2
    for k in range(CH):
        cols = slice(k * CW, (k + 1) * CW)
        whole(x_in.at[k], x_recv.at[k])
        for n in range(7):
            high, low = unpack(x_in[k, n, 0:half, :], x_in[k, n, half:half + 1, :], 1.0)
            x_part[n, 0:half, cols] = high
            x_part[n, half:, cols] = low
    whole(fac_in, f_recv)
    for k in range(CH):
        cols = slice(k * CW, (k + 1) * CW)
        part = weight * own_part[:, cols]
        for n in range(7):
            part = part + fac_in[n, 0:1, :] * x_part[n, :, cols]
        parts[:, cols] = part

    z_copies = []
    for d in Z_ORDER:
        words, level = pack(parts[d * ZR:(d + 1) * ZR, :])
        if d == 0:
            own_ref[0:6, :], own_ref[6:12, :] = unpack(words, level, 1.0)
            continue
        z_out[d - 1, 0:6, :] = words
        z_out[d - 1, 6:7, :] = level
        copy = pltpu.make_async_remote_copy(
            src_ref=z_out.at[d - 1], dst_ref=z_in.at[d - 1], send_sem=z_send, recv_sem=z_recv.at[d - 1],
            device_id=at_z(z_step(z) * d), device_id_type=MESH)
        copy.start()
        z_copies.append((d, copy))

    whole(p_out, p_send)
    whole(x_out, x_send)
    whole(stat_in, s_send)
    whole(fac_in, f_send)
    top_rows = low_rows = None
    for d, copy in reversed(z_copies):
        copy.wait_recv()
        words = z_in[d - 1]
        one, two = unpack(words[0:6], words[6:7], 1.0)
        top_rows = one if top_rows is None else top_rows + one
        low_rows = two if low_rows is None else low_rows + two
    rest_ref[0:6, :] = top_rows
    rest_ref[6:12, :] = low_rows

    whole(z_out, z_send)


def finish(own_ref, rest_ref, noise_ref, clip_ref, upd_ref, norm_ref):
    clipped = own_ref[...] + rest_ref[0:ZR, :]
    clip_ref[...] = clipped
    upd_ref[...] = (clipped + CLIP * noise_ref[...]) * (1.0 / IMAGES)
    norm_ref[0] = jnp.max(rest_ref[ZR:ZR + 1, 0:128])


def per_device(activations, out_grads, kept_mask, noise_field):
    vmem = pl.BlockSpec(memory_space=pltpu.VMEM)
    hbm = pl.BlockSpec(memory_space=pl.ANY)
    dma = pltpu.SemaphoreType.DMA
    bf16, f32, i32 = jnp.bfloat16, jnp.float32, jnp.int32
    own, rest = pl.pallas_call(
        kernel,
        out_shape=(jax.ShapeDtypeStruct((ZR, BW), f32), jax.ShapeDtypeStruct((16, BW), f32)),
        in_specs=[hbm, hbm, hbm],
        out_specs=(vmem,) * 2,
        scratch_shapes=[
            pltpu.VMEM((S, D), bf16),
            pltpu.VMEM((S, FF), bf16),
            pltpu.VMEM((1, 1), i32),
            pltpu.VMEM((4, 16, D), f32),
            pltpu.VMEM((3, 16, D), bf16),
            pltpu.VMEM((4, 16, D), bf16),
            pltpu.VMEM((4, SP, D), bf16),
            pltpu.VMEM((4 * SP, D), bf16),
            pltpu.VMEM((2, 4, SP, BW), bf16),
            pltpu.VMEM((D, D), bf16),
            pltpu.VMEM((D, BW), f32),
            pltpu.VMEM((CH, 2, D // 4 + 1, CW), i32),
            pltpu.VMEM((CH, 2, D // 4 + 1, CW), i32),
            pltpu.VMEM((XR, BW), f32),
            pltpu.VMEM((CH, 7, XR // 2 + 1, CW), i32),
            pltpu.VMEM((CH, 7, XR // 2 + 1, CW), i32),
            pltpu.VMEM((7, XR, BW), f32),
            pltpu.VMEM((XR, BW), f32),
            pltpu.VMEM((8, 128), f32),
            pltpu.VMEM((7, 8, 128), f32),
            pltpu.VMEM((8, 128), f32),
            pltpu.VMEM((7, 8, 128), f32),
            pltpu.VMEM((7, 7, BW), i32),
            pltpu.VMEM((7, 7, BW), i32),
            dma((6,)), dma, dma, dma, dma((3,)), dma, dma((CH + 1,)), dma, dma((CH, 2)), dma, dma((CH,)),
            dma, dma, dma, dma, dma, dma((7,)), pltpu.SemaphoreType.REGULAR((3,)),
        ],
        compiler_params=pltpu.CompilerParams(collective_id=0, has_side_effects=True, vmem_limit_bytes=53 * 2**20 + 700000),
        name="clipped_sum",
    )(activations[0, 0], out_grads[0, 0], kept_mask)
    clipped, update, norm = pl.pallas_call(
        finish,
        out_shape=(
            jax.ShapeDtypeStruct((ZR, BW), f32), jax.ShapeDtypeStruct((ZR, BW), f32), jax.ShapeDtypeStruct((1,), f32)),
        in_specs=[vmem] * 3,
        out_specs=(vmem, vmem, pl.BlockSpec(memory_space=pltpu.SMEM)),
        compiler_params=pltpu.CompilerParams(vmem_limit_bytes=2**20),
        name="update",
    )(own, rest, noise_field)
    return clipped, update, norm


def solution(mesh):
    in_specs = (
        P("img", "aug", None, None),
        P("img", "aug", None, None),
        P("img", "aug"),
        P("img", "aug"),
    )
    out_specs = (P("img", "aug"), P("img", "aug"), P("img"))
    return jax.shard_map(
        per_device, mesh=mesh, in_specs=in_specs, out_specs=out_specs, check_vma=False
    )
```
